32 devices in a mesh: group: 2 (over core), dp: 4 (over z), mp: 4 (over y, x).
Axes of the slice: x: 2, y: 2, z: 4, core: 2. Of those that a mesh axis runs over, the one named last changes fastest.
Arguments:
- kv_up_grads: bfloat16 [4096, 4096], P(('group', 'dp'), 'mp'), may hold values from -40 to 40
- tok_grads: bfloat16 [2048, 2048], P(('group', 'dp')), may hold values from -6 to 6
- token_rows: int32 [2048], P(('group', 'dp')), may hold values from 0 to 511
- step_count: int32 [1], replicated, may hold values from 1 to 11
- master: float32 [4, 786432], P('mp', 'dp'), may hold values from -0.12 to 0.12
- moment_one: float32 [4, 786432], P('mp', 'dp'), may hold values from -0.004 to 0.004
- moment_two: float32 [4, 786432], P('mp', 'dp'), may hold values from 1e-08 to 1e-06
- average: float32 [4, 786432], P('mp', 'dp'), may hold values from -0.12 to 0.12
Outputs:
- new_kv_up: bfloat16 [512, 4096], P(None, 'mp')
- new_embed: bfloat16 [512, 2048], P('mp')
- new_master: float32 [4, 786432], P('mp', 'dp')
- new_moment_one: float32 [4, 786432], P('mp', 'dp')
- new_moment_two: float32 [4, 786432], P('mp', 'dp')
- new_average: float32 [4, 786432], P('mp', 'dp')
The draws below stay inside these ranges and needn't reach their ends.
All inputs are finite; a program needn't handle non-finite values.
Results may differ from the reference program's by a relative error of at most 0.001.
Values may be sent and summed in bfloat16 or wider, within the bound.
No kernel may reach another device: no remote copies, remote signals or barrier semaphores. Data moves between devices by JAX's collectives and lax.ppermute only.
A program may use at most 64 MiB of HBM per device.

```python
import math
import jax
import jax.numpy as jnp
import numpy as np
from jax import lax

D = 2048
R = 512
EROWS = 512
TOKD = 256
HW = 4096
SH = 196608
TOKENS = 2048
N_GROUP = 2
N_DP = 4
N_MP = 4


SHOWN_NORM = 1.8275


def draw_kv_up_grads(key, part):
    shards = TOKENS // TOKD
    keys = jax.random.split(jax.random.fold_in(key, 17), 3)
    row_u = jax.random.uniform(keys[0], (R // 8,), jnp.float32, -1.5, 1.5)
    col_u = jax.random.uniform(keys[1], (16,), jnp.float32, -1.5, 1.5)
    row_level = jnp.repeat(jnp.exp(row_u) / SHOWN_NORM, 8)
    col_level = jnp.repeat(jnp.exp(col_u) / SHOWN_NORM, HW // 16)
    noise = jnp.clip(jax.random.normal(keys[2], (shards, R, HW), jnp.float32), -6.0, 6.0)
    value = noise * row_level[None, :, None] * col_level[None, None, :]
    return value.reshape(shards * R, HW).astype(jnp.bfloat16)


def plant(result, key, smallest, high):
    spot = [jax.random.randint(jax.random.fold_in(key, axis), (), 0, length) for axis, length in enumerate(result.shape)]
    longest = result.shape.index(max(result.shape))
    beside = spot[:longest] + [(spot[longest] + 1) % result.shape[longest]] + spot[longest + 1:]
    return result.at[tuple(spot)].set(smallest).at[tuple(beside)].set(high)


def shard_levels(key, extent, cuts, smallest, high):
    def one(position, parts):
        heights = jax.random.uniform(jax.random.fold_in(jax.random.fold_in(key, 6), position), (parts,), jnp.float32, smallest / len(cuts), high / len(cuts))
        return jnp.repeat(jnp.exp(heights), extent[position] // parts).reshape((-1,) + (1,) * (len(extent) - position - 1))

    gain = one(*cuts[0])
    for cut in cuts[1:]:
        gain = gain * one(*cut)
    return gain


def rank_bounds(number_of, lean):
    loads = [(1 << 20) // math.isqrt(rank ** lean) + 1 for rank in range(1, number_of + 1)]
    deviation = 1 + sum(loads) // (1 << 30)
    return np.cumsum(np.array([max(1, weight // deviation) for weight in loads]))


def skewed_ids(key, shape, amount, slope):
    grid = rank_bounds(amount, slope)
    lot = jax.random.randint(jax.random.fold_in(key, 1), shape, 0, int(grid[amount - 1]))
    standing = jnp.searchsorted(jnp.asarray(grid, jnp.int32), lot, side="right")
    return jax.random.permutation(jax.random.fold_in(key, 2), amount)[standing].astype(jnp.int32)


def centred(own_key, dims, scale, limit, pieces=(), dtype=jnp.bfloat16):
    level = shard_levels(own_key, dims, pieces, -0.22, 0.18) if pieces else 1.0
    drawn = jax.random.normal(own_key, dims, jnp.float32) * scale * level
    return jnp.minimum(jnp.maximum(drawn, -limit), limit).astype(dtype)


def setup_inputs(seed: int = 0) -> dict:
    key_of = jax.random.split(jax.random.key(seed), 9)
    return {
        "kv_up_grads": draw_kv_up_grads(jax.random.fold_in(key_of[8], 71), 0),
        "tok_grads": centred(key_of[1], (TOKENS, D), 1.0, 6.0, ((0, 8),)),
        "token_rows": plant(skewed_ids(key_of[2], (TOKENS,), EROWS, 2), jax.random.fold_in(key_of[2], 3), 0, EROWS - 1).astype(jnp.int32),
        "step_count": jax.random.randint(key_of[3], (1,), 1, 12).astype(jnp.int32),
        "master": centred(key_of[4], (N_MP, N_DP * SH), 0.02, 0.12, ((0, 4), (1, 4)), jnp.float32),
        "moment_one": centred(key_of[5], (N_MP, N_DP * SH), 0.0006, 0.004, ((0, 4), (1, 4)), jnp.float32),
        "moment_two": jnp.clip(jnp.exp(math.log(9.999999974752427e-07) - 4.6051702 * jax.random.uniform(key_of[6], (N_MP, N_DP * SH), jnp.float32) ** shard_levels(key_of[6], (N_MP, N_DP * SH), ((0, 4), (1, 4)), -0.2, 0.2)), 9.99999993922529e-09, 9.999999974752427e-07),
        "average": centred(key_of[7], (N_MP, N_DP * SH), 0.02, 0.12, ((0, 4), (1, 4)), jnp.float32),
    }


BETA_ONE = 0.9
BETA_TWO = 0.95
LEARN_RATE = 0.02
DECAY_RATE = 0.1
EPSILON = 1e-08
CLIP_NORM = 1.0
AVG_DECAY = 0.9

def to_state(latent, embed):
    block_cols = latent.shape[1] // N_MP
    latent_part = latent.reshape(R, N_MP, block_cols).transpose(1, 0, 2).reshape(N_MP, N_DP, -1)
    embed_part = embed.reshape(N_MP, N_DP, -1)
    return jnp.concatenate([latent_part, embed_part], axis=2).reshape(N_MP, -1)

def from_state(state):
    state_cube = state.reshape(N_MP, N_DP, -1)
    block_cols = HW // N_MP
    latent_len = R // N_DP * block_cols
    latent = state_cube[:, :, :latent_len].reshape(N_MP, R, block_cols).transpose(1, 0, 2).reshape(R, HW)
    embed = state_cube[:, :, latent_len:].reshape(EROWS, D)
    return (latent, embed)

def add_one(running, piece):
    return (running + piece.astype(jnp.float32), None)

def reference(kv_up_grads, tok_grads, token_rows, step_count, master, moment_one, moment_two, average):
    partials = kv_up_grads.reshape(N_GROUP * N_DP, R, HW)
    grad_kv, _ = lax.scan(add_one, jnp.zeros((R, HW), jnp.float32), partials)
    grad_embed = jax.ops.segment_sum(tok_grads.astype(jnp.float32), token_rows, num_segments=EROWS)
    gradient = to_state(grad_kv, grad_embed)
    norm_value = jnp.sqrt(jnp.sum(gradient * gradient))
    factor = CLIP_NORM / jnp.maximum(norm_value, CLIP_NORM)
    clipped = factor * gradient
    step_float = step_count[0].astype(jnp.float32)
    new_moment_one = BETA_ONE * moment_one + (1.0 - BETA_ONE) * clipped
    new_moment_two = BETA_TWO * moment_two + (1.0 - BETA_TWO) * clipped * clipped
    first_hat = new_moment_one / (1.0 - jnp.power(jnp.float32(BETA_ONE), step_float))
    second_hat = new_moment_two / (1.0 - jnp.power(jnp.float32(BETA_TWO), step_float))
    new_master = master - LEARN_RATE * (first_hat / (jnp.sqrt(second_hat) + EPSILON) + DECAY_RATE * master)
    new_average = AVG_DECAY * average + (1.0 - AVG_DECAY) * new_master
    new_kv_up, new_embed = from_state(new_master.astype(jnp.bfloat16))
    return (new_kv_up, new_embed, new_master, new_moment_one, new_moment_two, new_average)
```

```python
import functools

import jax
import jax.numpy as jnp
from jax import lax
from jax.experimental import pallas as pl
from jax.experimental.pallas import tpu as pltpu
from jax.sharding import PartitionSpec as P

EROWS = 512


BETA_ONE = 0.9
BETA_TWO = 0.95
LEARN_RATE = 0.02
DECAY_RATE = 0.1
EPSILON = 1e-08
CLIP_NORM = 1.0
AVG_DECAY = 0.9

LANES = 128
LATENT_SCALE = 512.0
EMBED_SCALE = 16.0


def embed_partial(token_rows, tok_grads):
    block_rows = EROWS // lax.axis_size("mp")
    slot_ids = lax.axis_index("mp") * block_rows + lax.iota(jnp.int32, block_rows)
    onehot = (slot_ids[:, None] == token_rows[None, :]).astype(jnp.bfloat16)
    return jnp.dot(onehot, tok_grads, preferred_element_type=jnp.float32)


def scalars(sum_squares, step_count):
    factor = CLIP_NORM / jnp.maximum(jnp.sqrt(sum_squares), CLIP_NORM)
    step_float = step_count[0].astype(jnp.float32)
    first_scale = 1.0 / (1.0 - jnp.power(jnp.float32(BETA_ONE), step_float))
    second_scale = 1.0 / (1.0 - jnp.power(jnp.float32(BETA_TWO), step_float))
    return factor, first_scale, second_scale


def adam(gradient, factor, first_scale, second_scale, master, moment_one, moment_two):
    clipped = factor * gradient
    new_one = BETA_ONE * moment_one + (1.0 - BETA_ONE) * clipped
    new_two = BETA_TWO * moment_two + (1.0 - BETA_TWO) * clipped * clipped
    step = (new_one * first_scale) / (jnp.sqrt(new_two * second_scale) + EPSILON)
    new_master = master - LEARN_RATE * (step + DECAY_RATE * master)
    return new_master, new_one, new_two


def weights_kernel(core_ref, scale_ref, latent_ref, embed_ref, master_ref, one_ref, two_ref, latent_out, embed_out):
    core = core_ref[0]
    first_row = 0
    for grad_ref, out_ref in ((latent_ref, latent_out), (embed_ref, embed_out)):
        rows, half = grad_ref.shape
        width = 2 * half // LANES
        for block in range(half // LANES):
            spot = pl.ds(first_row + core * (half // LANES) + block, rows, stride=width)
            columns = slice(block * LANES, (block + 1) * LANES)
            new_master, _, _ = adam(
                grad_ref[:, columns], scale_ref[0], scale_ref[1], scale_ref[2],
                master_ref[spot, :], one_ref[spot, :], two_ref[spot, :],
            )
            out_ref[:, columns] = new_master.astype(out_ref.dtype)
        first_row += rows * width


def state_kernel(core_ref, scale_ref, latent_mine, latent_other, embed_mine, embed_other,
                 master_ref, one_ref, two_ref, average_ref,
                 master_out, one_out, two_out, average_out, gradient):
    core = core_ref[0]
    first_row = 0
    for mine, other in ((latent_mine, latent_other), (embed_mine, embed_other)):
        rows, half = mine.shape
        blocks = half // LANES
        for ref, side in ((mine, core), (other, 1 - core)):
            for block in range(blocks):
                spot = pl.ds(first_row + side * blocks + block, rows, stride=2 * blocks)
                gradient[spot, :] = ref[:, block * LANES:(block + 1) * LANES]
        first_row += rows * 2 * blocks
    new_master, new_one, new_two = adam(
        gradient[...], scale_ref[0], scale_ref[1], scale_ref[2], master_ref[...], one_ref[...], two_ref[...]
    )
    master_out[...] = new_master
    one_out[...] = new_one
    two_out[...] = new_two
    average_out[...] = AVG_DECAY * average_ref[...] + (1.0 - AVG_DECAY) * new_master


def direct_shards(kv_up_grads, tok_grads, token_rows, step_count, master, moment_one, moment_two, average):
    n_dp = lax.axis_size("dp")
    core, me = lax.axis_index("group"), lax.axis_index("dp")
    swap = [(0, 1), (1, 0)]

    def half_of(array, side):
        half = array.shape[1] // 2
        return lax.dynamic_slice(array, (0, side * half), (array.shape[0], half))

    latent_got = lax.ppermute(half_of(kv_up_grads, 1 - core), "group", swap)
    rows_got = lax.ppermute(token_rows, "group", swap)
    tok_got = lax.ppermute(half_of(tok_grads, 1 - core), "group", swap)
    latent_mine = half_of(kv_up_grads, core)
    embed_pair = embed_partial(token_rows, half_of(tok_grads, core)) + embed_partial(rows_got, tok_got)

    latent_rows = kv_up_grads.shape[0] // n_dp
    embed_rows = embed_pair.shape[0] // n_dp

    def latent_block(owner):
        take = lambda array: lax.dynamic_slice_in_dim(array, owner * latent_rows, latent_rows, 0)
        return take(latent_mine).astype(jnp.float32) + take(latent_got).astype(jnp.float32)

    def embed_block(owner):
        return lax.dynamic_slice_in_dim(embed_pair, owner * embed_rows, embed_rows, 0)

    def exchange(block_of, scale):
        got = []
        for step in range(n_dp - 1, 0, -1):
            block = (block_of(me ^ step) * scale).astype(jnp.float16)
            got.append(lax.ppermute(block, "dp", [(i, i ^ step) for i in range(n_dp)]))
        total = got[0].astype(jnp.float32)
        for block in got[1:]:
            total = total + block.astype(jnp.float32)
        return block_of(me) + total * (1.0 / scale)

    latent_sum = exchange(latent_block, LATENT_SCALE)
    embed_sum = exchange(embed_block, EMBED_SCALE)

    squares = jnp.sum(latent_sum * latent_sum) + jnp.sum(embed_sum * embed_sum)
    everyone = ("group", "dp", "mp")
    n_all = lax.axis_size(everyone)
    squares = lax.all_to_all(jnp.broadcast_to(squares, (n_all, LANES)), everyone, 0, 0, tiled=True)
    factors = jnp.stack(scalars(jnp.sum(squares[:, 0]), step_count))
    core_word = core.astype(jnp.int32).reshape(1)

    flat = lambda array: array.reshape(-1, LANES)
    states = [flat(array) for array in (master, moment_one, moment_two, average)]
    smem = pl.BlockSpec(memory_space=pltpu.SMEM)
    vmem = pl.BlockSpec(memory_space=pltpu.VMEM)

    weights = pl.pallas_call(
        weights_kernel,
        out_shape=[jax.ShapeDtypeStruct(a.shape, jnp.bfloat16) for a in (latent_sum, embed_sum)],
        in_specs=[smem] * 2 + [vmem] * 5,
        out_specs=[vmem] * 2,
        compiler_params=pltpu.CompilerParams(vmem_limit_bytes=16 << 20),
        name="weights",
    )(core_word, factors, latent_sum, embed_sum, *states[:3])

    def gather(block):
        half = block.shape[1]
        out = jnp.zeros((n_dp * block.shape[0], 2 * half), block.dtype)
        for step in range(n_dp - 1, -1, -1):
            mine = block
            if step:
                mine = lax.ppermute(block, "dp", [(i, i ^ step) for i in range(n_dp)])
            other = lax.ppermute(mine, "group", swap)
            row = (me ^ step) * block.shape[0]
            out = lax.dynamic_update_slice(out, mine, (row, core * half))
            out = lax.dynamic_update_slice(out, other, (row, (1 - core) * half))
        return out

    new_kv_up, new_embed = gather(weights[0]), gather(weights[1])

    latent_other = lax.ppermute(latent_sum, "group", swap)
    embed_other = lax.ppermute(embed_sum, "group", swap)
    new_state = pl.pallas_call(
        state_kernel,
        out_shape=[jax.ShapeDtypeStruct(states[0].shape, jnp.float32)] * 4,
        in_specs=[smem] * 2 + [vmem] * 8,
        out_specs=[vmem] * 4,
        scratch_shapes=[pltpu.VMEM(states[0].shape, jnp.float32)],
        compiler_params=pltpu.CompilerParams(vmem_limit_bytes=24 << 20),
        name="state",
    )(core_word, factors, latent_sum, latent_other, embed_sum, embed_other, *states)
    return (new_kv_up, new_embed, *[array.reshape(master.shape) for array in new_state])


def scattered_shards(kv_up_grads, tok_grads, token_rows, step_count, master, moment_one, moment_two, average):
    latent_part = kv_up_grads.astype(jnp.float32)
    embed_part = embed_partial(token_rows, tok_grads)
    latent_rows, embed_rows = (
        lax.psum_scatter(latent_part, "dp", scatter_dimension=0, tiled=True),
        lax.psum_scatter(embed_part, "dp", scatter_dimension=0, tiled=True),
    )
    latent_rows, embed_rows = lax.psum((latent_rows, embed_rows), "group")
    gradient = jnp.concatenate([latent_rows.reshape(1, -1), embed_rows.reshape(1, -1)], axis=1)
    sum_squares = lax.psum(jnp.sum(gradient * gradient), ("dp", "mp"))
    new_master, new_one, new_two = adam(
        gradient, *scalars(sum_squares, step_count), master, moment_one, moment_two
    )
    new_average = AVG_DECAY * average + (1.0 - AVG_DECAY) * new_master
    weights = new_master.astype(jnp.bfloat16)
    latent_len = latent_rows.shape[0] * latent_rows.shape[1]
    latent_new = weights[0, :latent_len].reshape(latent_rows.shape)
    embed_new = weights[0, latent_len:].reshape(embed_rows.shape)
    new_kv_up, new_embed = (
        lax.all_gather(latent_new, "dp", axis=0, tiled=True),
        lax.all_gather(embed_new, "dp", axis=0, tiled=True),
    )
    return (new_kv_up, new_embed, new_master, new_one, new_two, new_average)


def solution(mesh):
    placed = (
        P(("group", "dp"), "mp"),
        P(("group", "dp"), None),
        P(("group", "dp")),
        P(),
        P("mp", "dp"),
        P("mp", "dp"),
        P("mp", "dp"),
        P("mp", "dp"),
    )
    few = mesh.shape["group"] == 2 and mesh.shape["dp"] in (2, 4)
    return jax.shard_map(
        direct_shards if few else scattered_shards,
        mesh=mesh,
        in_specs=placed,
        out_specs=(
            P(None, "mp"),
            P("mp", None),
            P("mp", "dp"),
            P("mp", "dp"),
            P("mp", "dp"),
            P("mp", "dp"),
        ),
        check_vma=False,
    )
```

```python
import functools

import jax
import jax.numpy as jnp
from jax import lax
from jax.experimental import pallas as pl
from jax.experimental.pallas import tpu as pltpu
from jax.sharding import PartitionSpec as P

EROWS = 512


BETA_ONE = 0.9
BETA_TWO = 0.95
LEARN_RATE = 0.02
DECAY_RATE = 0.1
EPSILON = 1e-08
CLIP_NORM = 1.0
AVG_DECAY = 0.9

LANES = 128
LATENT_SCALE = 512.0
EMBED_SCALE = 16.0


def embed_partial(token_rows, tok_grads):
    block_rows = EROWS // lax.axis_size("mp")
    slot_ids = lax.axis_index("mp") * block_rows + lax.iota(jnp.int32, block_rows)
    onehot = (slot_ids[:, None] == token_rows[None, :]).astype(jnp.bfloat16)
    return jnp.dot(onehot, tok_grads, preferred_element_type=jnp.float32)


def step_scales(step_count):
    step_float = step_count[0].astype(jnp.float32)
    first_scale = 1.0 / (1.0 - jnp.power(jnp.float32(BETA_ONE), step_float))
    second_scale = 1.0 / (1.0 - jnp.power(jnp.float32(BETA_TWO), step_float))
    return first_scale, second_scale


def clip_factor(sum_squares):
    return CLIP_NORM / jnp.maximum(jnp.sqrt(sum_squares), CLIP_NORM)


def adam(gradient, factor, first_scale, second_scale, master, moment_one, moment_two):
    clipped = factor * gradient
    new_one = BETA_ONE * moment_one + (1.0 - BETA_ONE) * clipped
    new_two = BETA_TWO * moment_two + (1.0 - BETA_TWO) * clipped * clipped
    step = (new_one * first_scale) / (jnp.sqrt(new_two * second_scale) + EPSILON)
    new_master = master - LEARN_RATE * (step + DECAY_RATE * master)
    return new_master, new_one, new_two


def total_factor(squares_ref):
    squares = jnp.sum(squares_ref[...], axis=0, keepdims=True)
    return clip_factor(jnp.sum(squares, axis=1, keepdims=True))


def weights_kernel(core_ref, scale_ref, squares_ref, latent_ref, embed_ref, master_ref, one_ref, two_ref, packed_ref):
    core = core_ref[0]
    factor = total_factor(squares_ref)
    packed_width = packed_ref.shape[1]
    first_row = out_row = 0
    for grad_ref in (latent_ref, embed_ref):
        rows, half = grad_ref.shape
        width = 2 * half // LANES
        for block in range(half // LANES):
            spot = pl.ds(first_row + core * (half // LANES) + block, rows, stride=width)
            new_master, _, _ = adam(
                grad_ref[:, block * LANES:(block + 1) * LANES], factor, scale_ref[0], scale_ref[1],
                master_ref[spot, :], one_ref[spot, :], two_ref[spot, :],
            )
            stretch, column = divmod(block * LANES, packed_width)
            row = out_row + stretch * rows
            packed_ref[row:row + rows, column:column + LANES] = new_master.astype(packed_ref.dtype)
        first_row += rows * width
        out_row += rows * (half // packed_width)


def state_kernel(core_ref, scale_ref, squares_ref, latent_mine, latent_other, embed_mine, embed_other,
                 master_ref, one_ref, two_ref, average_ref,
                 master_out, one_out, two_out, average_out, gradient):
    core = core_ref[0]
    first_row = 0
    for mine, other in ((latent_mine, latent_other), (embed_mine, embed_other)):
        rows, half = mine.shape
        blocks = half // LANES
        for ref, side in ((mine, core), (other, 1 - core)):
            for block in range(blocks):
                spot = pl.ds(first_row + side * blocks + block, rows, stride=2 * blocks)
                gradient[spot, :] = ref[:, block * LANES:(block + 1) * LANES]
        first_row += rows * 2 * blocks
    new_master, new_one, new_two = adam(
        gradient[...], total_factor(squares_ref), scale_ref[0], scale_ref[1],
        master_ref[...], one_ref[...], two_ref[...],
    )
    master_out[...] = new_master
    one_out[...] = new_one
    two_out[...] = new_two
    average_out[...] = AVG_DECAY * average_ref[...] + (1.0 - AVG_DECAY) * new_master


def assemble_kernel(latent_rows, embed_rows, place_ref, *refs):
    *pieces, latent_out, embed_out, sems = refs
    core, me = place_ref[0], place_ref[1]
    n_dp = len(pieces) // 2
    width = pieces[0].shape[1]
    stretches = (pieces[0].shape[0] - latent_rows) // embed_rows
    copies = []

    def put(source, target):
        copies.append(pltpu.make_async_copy(source, target, sems.at[len(copies)]))
        copies[-1].start()

    for step in range(n_dp):
        owner = me ^ step
        latent_row = pl.multiple_of(owner * latent_rows, latent_rows)
        embed_row = pl.multiple_of(owner * embed_rows, embed_rows)
        for piece, side in ((pieces[2 * step], core), (pieces[2 * step + 1], 1 - core)):
            column = pl.multiple_of(side * width, width)
            put(piece.at[pl.ds(0, latent_rows)], latent_out.at[pl.ds(latent_row, latent_rows), pl.ds(column, width)])
            for stretch in range(stretches):
                column = pl.multiple_of((side * stretches + stretch) * width, width)
                put(
                    piece.at[pl.ds(latent_rows + stretch * embed_rows, embed_rows)],
                    embed_out.at[pl.ds(embed_row, embed_rows), pl.ds(column, width)],
                )
    for copy in copies:
        copy.wait()


def direct_shards(kv_up_grads, tok_grads, token_rows, step_count, master, moment_one, moment_two, average):
    n_dp = lax.axis_size("dp")
    core, me = lax.axis_index("group"), lax.axis_index("dp")
    swap = [(0, 1), (1, 0)]

    def half_of(array, side):
        half = array.shape[1] // 2
        return lax.dynamic_slice(array, (0, side * half), (array.shape[0], half))

    latent_got = lax.ppermute(half_of(kv_up_grads, 1 - core), "group", swap)
    rows_got = lax.ppermute(token_rows, "group", swap)
    tok_got = lax.ppermute(half_of(tok_grads, 1 - core), "group", swap)
    latent_mine = half_of(kv_up_grads, core)
    embed_pair = embed_partial(token_rows, half_of(tok_grads, core)) + embed_partial(rows_got, tok_got)

    latent_rows = kv_up_grads.shape[0] // n_dp
    embed_rows = embed_pair.shape[0] // n_dp

    def latent_block(owner):
        take = lambda array: lax.dynamic_slice_in_dim(array, owner * latent_rows, latent_rows, 0)
        return take(latent_mine).astype(jnp.float32) + take(latent_got).astype(jnp.float32)

    def embed_block(owner):
        return lax.dynamic_slice_in_dim(embed_pair, owner * embed_rows, embed_rows, 0)

    def exchange(block_of, scale):
        got = []
        for step in range(n_dp - 1, 0, -1):
            block = (block_of(me ^ step) * scale).astype(jnp.float16)
            got.append(lax.ppermute(block, "dp", [(i, i ^ step) for i in range(n_dp)]))
        total = got[0].astype(jnp.float32)
        for block in got[1:]:
            total = total + block.astype(jnp.float32)
        return block_of(me) + total * (1.0 / scale)

    latent_sum = exchange(latent_block, LATENT_SCALE)
    embed_sum = exchange(embed_block, EMBED_SCALE)

    width = latent_sum.shape[1]
    squares = jnp.sum(latent_sum * latent_sum, axis=0)
    embed_squares = jnp.sum(embed_sum * embed_sum, axis=0)
    for stretch in range(embed_sum.shape[1] // width):
        squares = squares + embed_squares[stretch * width:(stretch + 1) * width]
    everyone = ("group", "dp", "mp")
    n_all = lax.axis_size(everyone)
    squares = lax.all_to_all(jnp.broadcast_to(squares, (n_all, width)), everyone, 0, 0, tiled=True)
    scales = jnp.stack(step_scales(step_count))
    place = jnp.stack([core, me]).astype(jnp.int32)

    flat = lambda array: array.reshape(-1, LANES)
    states = [flat(array) for array in (master, moment_one, moment_two, average)]
    smem = pl.BlockSpec(memory_space=pltpu.SMEM)
    vmem = pl.BlockSpec(memory_space=pltpu.VMEM)
    anywhere = pl.BlockSpec(memory_space=pl.ANY)

    packed_rows = latent_rows + embed_sum.size // width
    packed = pl.pallas_call(
        weights_kernel,
        out_shape=jax.ShapeDtypeStruct((packed_rows, width), jnp.bfloat16),
        in_specs=[smem] * 2 + [vmem] * 6,
        out_specs=vmem,
        compiler_params=pltpu.CompilerParams(vmem_limit_bytes=8 << 20),
        name="weights",
    )(place, scales, squares, latent_sum, embed_sum, *states[:3])

    pieces = []
    for step in range(n_dp):
        mine = packed
        if step:
            mine = lax.ppermute(packed, "dp", [(i, i ^ step) for i in range(n_dp)])
        pieces += [mine, lax.ppermute(mine, "group", swap)]

    latent_other = lax.ppermute(latent_sum, "group", swap)
    embed_other = lax.ppermute(embed_sum, "group", swap)
    entries = states[0].size
    new_state = pl.pallas_call(
        state_kernel,
        out_shape=[jax.ShapeDtypeStruct(states[0].shape, jnp.float32)] * 4,
        in_specs=[smem] * 2 + [vmem] * 9,
        out_specs=[vmem] * 4,
        scratch_shapes=[pltpu.VMEM(states[0].shape, jnp.float32)],
        compiler_params=pltpu.CompilerParams(vmem_limit_bytes=16 << 20),
        cost_estimate=pl.CostEstimate(flops=30 * entries, bytes_accessed=36 * entries, transcendentals=2 * entries),
        name="state",
    )(place, scales, squares, latent_sum, latent_other, embed_sum, embed_other, *states)

    new_kv_up, new_embed = pl.pallas_call(
        functools.partial(assemble_kernel, latent_rows, embed_rows),
        out_shape=[
            jax.ShapeDtypeStruct(kv_up_grads.shape, jnp.bfloat16),
            jax.ShapeDtypeStruct((n_dp * embed_rows, tok_grads.shape[1]), jnp.bfloat16),
        ],
        in_specs=[smem] + [anywhere] * len(pieces),
        out_specs=[anywhere] * 2,
        scratch_shapes=[pltpu.SemaphoreType.DMA((len(pieces) * (1 + embed_sum.shape[1] // width),))],
        name="assemble",
    )(place, *pieces)
    return (new_kv_up, new_embed, *[array.reshape(master.shape) for array in new_state])


def scattered_shards(kv_up_grads, tok_grads, token_rows, step_count, master, moment_one, moment_two, average):
    latent_part = kv_up_grads.astype(jnp.float32)
    embed_part = embed_partial(token_rows, tok_grads)
    latent_rows, embed_rows = (
        lax.psum_scatter(latent_part, "dp", scatter_dimension=0, tiled=True),
        lax.psum_scatter(embed_part, "dp", scatter_dimension=0, tiled=True),
    )
    latent_rows, embed_rows = lax.psum((latent_rows, embed_rows), "group")
    gradient = jnp.concatenate([latent_rows.reshape(1, -1), embed_rows.reshape(1, -1)], axis=1)
    sum_squares = lax.psum(jnp.sum(gradient * gradient), ("dp", "mp"))
    new_master, new_one, new_two = adam(
        gradient, clip_factor(sum_squares), *step_scales(step_count), master, moment_one, moment_two
    )
    new_average = AVG_DECAY * average + (1.0 - AVG_DECAY) * new_master
    weights = new_master.astype(jnp.bfloat16)
    latent_len = latent_rows.shape[0] * latent_rows.shape[1]
    latent_new = weights[0, :latent_len].reshape(latent_rows.shape)
    embed_new = weights[0, latent_len:].reshape(embed_rows.shape)
    new_kv_up, new_embed = (
        lax.all_gather(latent_new, "dp", axis=0, tiled=True),
        lax.all_gather(embed_new, "dp", axis=0, tiled=True),
    )
    return (new_kv_up, new_embed, new_master, new_one, new_two, new_average)


def solution(mesh):
    placed = (
        P(("group", "dp"), "mp"),
        P(("group", "dp"), None),
        P(("group", "dp")),
        P(),
        P("mp", "dp"),
        P("mp", "dp"),
        P("mp", "dp"),
        P("mp", "dp"),
    )
    few = mesh.shape["group"] == 2 and mesh.shape["dp"] in (2, 4)
    return jax.shard_map(
        direct_shards if few else scattered_shards,
        mesh=mesh,
        in_specs=placed,
        out_specs=(
            P(None, "mp"),
            P("mp", None),
            P("mp", "dp"),
            P("mp", "dp"),
            P("mp", "dp"),
            P("mp", "dp"),
        ),
        check_vma=False,
    )
```

```python
import functools

import jax
import jax.numpy as jnp
from jax import lax
from jax.experimental import pallas as pl
from jax.experimental.pallas import tpu as pltpu
from jax.sharding import PartitionSpec as P

EROWS = 512


BETA_ONE = 0.9
BETA_TWO = 0.95
LEARN_RATE = 0.02
DECAY_RATE = 0.1
EPSILON = 1e-08
CLIP_NORM = 1.0
AVG_DECAY = 0.9

SUBLANES = 8
LANES = 128
LATENT_SCALE = 512.0
EMBED_SCALE = 16.0


def embed_partial(token_rows, tok_grads):
    block_rows = EROWS // lax.axis_size("mp")
    slot_ids = lax.axis_index("mp") * block_rows + lax.iota(jnp.int32, block_rows)
    onehot = (slot_ids[:, None] == token_rows[None, :]).astype(jnp.bfloat16)
    return jnp.dot(onehot, tok_grads, preferred_element_type=jnp.float32)


def step_scales(step_count):
    step_float = step_count[0].astype(jnp.float32)
    first_scale = 1.0 / (1.0 - jnp.power(jnp.float32(BETA_ONE), step_float))
    second_scale = 1.0 / (1.0 - jnp.power(jnp.float32(BETA_TWO), step_float))
    return first_scale, second_scale


def clip_factor(sum_squares):
    return CLIP_NORM / jnp.maximum(jnp.sqrt(sum_squares), CLIP_NORM)


def adam(gradient, factor, first_scale, second_scale, master, moment_one, moment_two):
    clipped = factor * gradient
    new_one = BETA_ONE * moment_one + (1.0 - BETA_ONE) * clipped
    new_two = BETA_TWO * moment_two + (1.0 - BETA_TWO) * clipped * clipped
    step = (new_one * first_scale) / (jnp.sqrt(new_two * second_scale) + EPSILON)
    new_master = master - LEARN_RATE * (step + DECAY_RATE * master)
    return new_master, new_one, new_two


def total_factor(squares_ref):
    squares = jnp.sum(squares_ref[...], axis=0, keepdims=True)
    return clip_factor(jnp.sum(squares, axis=1, keepdims=True))


def weights_kernel(core_ref, scale_ref, squares_ref, latent_ref, embed_ref, master_ref, one_ref, two_ref, packed_ref):
    core = core_ref[0]
    factor = total_factor(squares_ref)
    packed_width = packed_ref.shape[1]
    first_row = out_row = 0
    for grad_ref in (latent_ref, embed_ref):
        rows, half = grad_ref.shape
        width = 2 * half // LANES
        for block in range(half // LANES):
            spot = pl.ds(first_row + core * (half // LANES) + block, rows, stride=width)
            new_master, _, _ = adam(
                grad_ref[:, block * LANES:(block + 1) * LANES], factor, scale_ref[0], scale_ref[1],
                master_ref[spot, :], one_ref[spot, :], two_ref[spot, :],
            )
            stretch, column = divmod(block * LANES, packed_width)
            row = out_row + stretch * rows
            packed_ref[row:row + rows, column:column + LANES] = new_master.astype(packed_ref.dtype)
        first_row += rows * width
        out_row += rows * (half // packed_width)


def state_kernel(core_ref, scale_ref, squares_ref, latent_mine, latent_other, embed_mine, embed_other,
                 master_ref, one_ref, two_ref, average_ref,
                 master_out, one_out, two_out, average_out, gradient):
    core = core_ref[0]
    first_row = 0
    for mine, other in ((latent_mine, latent_other), (embed_mine, embed_other)):
        rows, half = mine.shape
        blocks = half // LANES
        for ref, side in ((mine, core), (other, 1 - core)):
            for block in range(blocks):
                spot = pl.ds(first_row + side * blocks + block, rows, stride=2 * blocks)
                gradient[spot, :] = ref[:, block * LANES:(block + 1) * LANES]
        first_row += rows * 2 * blocks
    new_master, new_one, new_two = adam(
        gradient[...], total_factor(squares_ref), scale_ref[0], scale_ref[1],
        master_ref[...], one_ref[...], two_ref[...],
    )
    master_out[...] = new_master
    one_out[...] = new_one
    two_out[...] = new_two
    average_out[...] = AVG_DECAY * average_ref[...] + (1.0 - AVG_DECAY) * new_master


def assemble_kernel(latent_rows, embed_rows, place_ref, *refs):
    *pieces, latent_out, embed_out = refs
    left_is_mine = place_ref[0] == 0
    width = pieces[0].shape[1]
    stretches = (pieces[0].shape[0] - latent_rows) // embed_rows
    for step in range(len(pieces) // 2):
        owner = place_ref[1] ^ step
        latent_spot = pl.ds(pl.multiple_of(owner * latent_rows, latent_rows), latent_rows)
        embed_spot = pl.ds(pl.multiple_of(owner * embed_rows, embed_rows), embed_rows)
        mine, other = pieces[2 * step], pieces[2 * step + 1]

        def put(out_ref, spot, column, rows):
            half = out_ref.shape[1] // 2
            left = jnp.where(left_is_mine, mine[rows, :], other[rows, :])
            right = jnp.where(left_is_mine, other[rows, :], mine[rows, :])
            out_ref[spot, column:column + width] = left
            out_ref[spot, half + column:half + column + width] = right

        put(latent_out, latent_spot, 0, slice(0, latent_rows))
        for stretch in range(stretches):
            row = latent_rows + stretch * embed_rows
            put(embed_out, embed_spot, stretch * width, slice(row, row + embed_rows))


def direct_shards(kv_up_grads, tok_grads, token_rows, step_count, master, moment_one, moment_two, average):
    n_dp = lax.axis_size("dp")
    core, me = lax.axis_index("group"), lax.axis_index("dp")
    swap = [(0, 1), (1, 0)]

    def half_of(array, side):
        half = array.shape[1] // 2
        return lax.dynamic_slice(array, (0, side * half), (array.shape[0], half))

    latent_got = lax.ppermute(kv_up_grads, "group", swap)
    rows_got = lax.ppermute(token_rows, "group", swap)
    tok_got = lax.ppermute(half_of(tok_grads, 1 - core), "group", swap)

    latent_rows = kv_up_grads.shape[0] // n_dp
    half = kv_up_grads.shape[1] // 2

    def latent_block(owner):
        take = lambda array: lax.dynamic_slice(array, (owner * latent_rows, core * half), (latent_rows, half))
        return take(kv_up_grads).astype(jnp.float32) + take(latent_got).astype(jnp.float32)

    steps = [step for step in (2, 3, 1) if step < n_dp]

    def blocks_to_send(block_of, scale):
        return [(block_of(me ^ step) * scale).astype(jnp.float16) for step in steps]

    def summed(own, blocks, scale):
        got = [
            lax.ppermute(block, "dp", [(i, i ^ step) for i in range(n_dp)]).astype(jnp.float32)
            for step, block in zip(steps, blocks)
        ]
        return own + sum(got[1:], got[0]) * (1.0 / scale)

    latent_blocks = blocks_to_send(latent_block, LATENT_SCALE)
    latent_blocks, token_rows = lax.optimization_barrier((latent_blocks, token_rows))
    latent_sum = summed(latent_block(me), latent_blocks, LATENT_SCALE)

    embed_pair = embed_partial(token_rows, half_of(tok_grads, core)) + embed_partial(rows_got, tok_got)
    embed_rows = embed_pair.shape[0] // n_dp

    def embed_block(owner):
        return lax.dynamic_slice_in_dim(embed_pair, owner * embed_rows, embed_rows, 0)

    embed_sum = summed(embed_block(me), blocks_to_send(embed_block, EMBED_SCALE), EMBED_SCALE)

    def squares_of(array):
        tile = (array * array).reshape(-1, SUBLANES, array.shape[1]).sum(axis=0)
        return sum(tile[:, i:i + LANES] for i in range(0, array.shape[1], LANES))

    squares = squares_of(latent_sum) + squares_of(embed_sum)
    everyone = ("group", "dp", "mp")
    n_all = lax.axis_size(everyone)
    squares = lax.all_to_all(jnp.tile(squares, (n_all, 1)), everyone, 0, 0, tiled=True)
    scales = jnp.stack(step_scales(step_count))
    place = jnp.stack([core, me]).astype(jnp.int32)

    flat = lambda array: array.reshape(-1, LANES)
    states = [flat(array) for array in (master, moment_one, moment_two, average)]
    smem = pl.BlockSpec(memory_space=pltpu.SMEM)
    vmem = pl.BlockSpec(memory_space=pltpu.VMEM)

    packed_rows = latent_rows + embed_sum.size // half
    packed = pl.pallas_call(
        weights_kernel,
        out_shape=jax.ShapeDtypeStruct((packed_rows, half), jnp.bfloat16),
        in_specs=[smem] * 2 + [vmem] * 6,
        out_specs=vmem,
        compiler_params=pltpu.CompilerParams(vmem_limit_bytes=8 << 20),
        name="weights",
    )(place, scales, squares, latent_sum, embed_sum, *states[:3])

    latent_other = lax.ppermute(latent_sum, "group", swap)
    embed_other = lax.ppermute(embed_sum, "group", swap)
    gathered = {0: packed}
    for step in steps:
        gathered[step] = lax.ppermute(packed, "dp", [(i, i ^ step) for i in range(n_dp)])

    entries = states[0].size
    new_state = pl.pallas_call(
        state_kernel,
        out_shape=[jax.ShapeDtypeStruct(states[0].shape, jnp.float32)] * 4,
        in_specs=[smem] * 2 + [vmem] * 9,
        out_specs=[vmem] * 4,
        scratch_shapes=[pltpu.VMEM(states[0].shape, jnp.float32)],
        compiler_params=pltpu.CompilerParams(vmem_limit_bytes=16 << 20),
        cost_estimate=pl.CostEstimate(flops=30 * entries, bytes_accessed=36 * entries, transcendentals=2 * entries),
        name="state",
    )(place, scales, squares, latent_sum, latent_other, embed_sum, embed_other, *states)
    new_state, gathered = lax.optimization_barrier((new_state, gathered))

    pieces = []
    for step in range(n_dp):
        pieces += [gathered[step], lax.ppermute(gathered[step], "group", swap)]
    new_kv_up, new_embed = pl.pallas_call(
        functools.partial(assemble_kernel, latent_rows, embed_rows),
        out_shape=[
            jax.ShapeDtypeStruct(kv_up_grads.shape, jnp.bfloat16),
            jax.ShapeDtypeStruct((n_dp * embed_rows, tok_grads.shape[1]), jnp.bfloat16),
        ],
        in_specs=[smem] + [vmem] * len(pieces),
        out_specs=[vmem] * 2,
        compiler_params=pltpu.CompilerParams(vmem_limit_bytes=8 << 20),
        name="assemble",
    )(place, *pieces)
    return (new_kv_up, new_embed, *[array.reshape(master.shape) for array in new_state])


def scattered_shards(kv_up_grads, tok_grads, token_rows, step_count, master, moment_one, moment_two, average):
    latent_part = kv_up_grads.astype(jnp.float32)
    embed_part = embed_partial(token_rows, tok_grads)
    latent_rows, embed_rows = (
        lax.psum_scatter(latent_part, "dp", scatter_dimension=0, tiled=True),
        lax.psum_scatter(embed_part, "dp", scatter_dimension=0, tiled=True),
    )
    latent_rows, embed_rows = lax.psum((latent_rows, embed_rows), "group")
    gradient = jnp.concatenate([latent_rows.reshape(1, -1), embed_rows.reshape(1, -1)], axis=1)
    sum_squares = lax.psum(jnp.sum(gradient * gradient), ("dp", "mp"))
    new_master, new_one, new_two = adam(
        gradient, clip_factor(sum_squares), *step_scales(step_count), master, moment_one, moment_two
    )
    new_average = AVG_DECAY * average + (1.0 - AVG_DECAY) * new_master
    weights = new_master.astype(jnp.bfloat16)
    latent_len = latent_rows.shape[0] * latent_rows.shape[1]
    latent_new = weights[0, :latent_len].reshape(latent_rows.shape)
    embed_new = weights[0, latent_len:].reshape(embed_rows.shape)
    new_kv_up, new_embed = (
        lax.all_gather(latent_new, "dp", axis=0, tiled=True),
        lax.all_gather(embed_new, "dp", axis=0, tiled=True),
    )
    return (new_kv_up, new_embed, new_master, new_one, new_two, new_average)


def solution(mesh):
    placed = (
        P(("group", "dp"), "mp"),
        P(("group", "dp"), None),
        P(("group", "dp")),
        P(),
        P("mp", "dp"),
        P("mp", "dp"),
        P("mp", "dp"),
        P("mp", "dp"),
    )
    few = mesh.shape["group"] == 2 and mesh.shape["dp"] in (2, 4)
    return jax.shard_map(
        direct_shards if few else scattered_shards,
        mesh=mesh,
        in_specs=placed,
        out_specs=(
            P(None, "mp"),
            P("mp", None),
            P("mp", "dp"),
            P("mp", "dp"),
            P("mp", "dp"),
            P("mp", "dp"),
        ),
        check_vma=False,
    )
```

```python
import functools

import jax
import jax.numpy as jnp
from jax import lax
from jax.experimental import pallas as pl
from jax.experimental.pallas import tpu as pltpu
from jax.sharding import PartitionSpec as P

EROWS = 512


BETA_ONE = 0.9
BETA_TWO = 0.95
LEARN_RATE = 0.02
DECAY_RATE = 0.1
EPSILON = 1e-08
CLIP_NORM = 1.0
AVG_DECAY = 0.9

SUBLANES = 8
LANES = 128
LATENT_SCALE = 512.0
EMBED_SCALE = 16.0


def embed_partial(token_rows, tok_grads):
    block_rows = EROWS // lax.axis_size("mp")
    slot_ids = lax.axis_index("mp") * block_rows + lax.iota(jnp.int32, block_rows)
    onehot = (slot_ids[:, None] == token_rows[None, :]).astype(jnp.bfloat16)
    return jnp.dot(onehot, tok_grads, preferred_element_type=jnp.float32)


def step_scales(step_count):
    step_float = step_count[0].astype(jnp.float32)
    first_scale = 1.0 / (1.0 - jnp.power(jnp.float32(BETA_ONE), step_float))
    second_scale = 1.0 / (1.0 - jnp.power(jnp.float32(BETA_TWO), step_float))
    return first_scale, second_scale


def clip_factor(sum_squares):
    return CLIP_NORM / jnp.maximum(jnp.sqrt(sum_squares), CLIP_NORM)


def adam(gradient, factor, first_scale, second_scale, master, moment_one, moment_two):
    clipped = factor * gradient
    new_one = BETA_ONE * moment_one + (1.0 - BETA_ONE) * clipped
    new_two = BETA_TWO * moment_two + (1.0 - BETA_TWO) * clipped * clipped
    step = (new_one * first_scale) / (jnp.sqrt(new_two * second_scale) + EPSILON)
    new_master = master - LEARN_RATE * (step + DECAY_RATE * master)
    return new_master, new_one, new_two


def total_factor(squares_ref):
    squares = jnp.sum(squares_ref[...], axis=0, keepdims=True)
    return clip_factor(jnp.sum(squares, axis=1, keepdims=True))


def packed_slots(latent_shape, embed_shape):
    latent_rows, width = latent_shape
    embed_rows, embed_half = embed_shape
    for column in range(0, width, LANES):
        yield False, column, slice(0, latent_rows), slice(column, column + LANES)
    for column in range(0, embed_half, LANES):
        row = latent_rows + column // width * embed_rows
        yield True, column, slice(row, row + embed_rows), slice(column % width, column % width + LANES)


def load(sources, targets, sems):
    copies = [pltpu.make_async_copy(*pair, sems.at[i]) for i, pair in enumerate(zip(sources, targets))]
    for copy in copies:
        copy.start()
    for copy in copies:
        copy.wait()


def pick_kernel(latent_shape, embed_shape, place_ref, master_ref, one_ref, two_ref, *refs):
    packed_ref, master, one, two, sems = refs
    load((master_ref, one_ref, two_ref), (master, one, two), sems)
    core = place_ref[0]
    for is_embed, column, rows, columns in packed_slots(latent_shape, embed_shape):
        height, half = embed_shape if is_embed else latent_shape
        start = latent_shape[0] * 2 * latent_shape[1] // LANES if is_embed else 0
        spot = pl.ds(start + core * (half // LANES) + column // LANES, height, stride=2 * half // LANES)
        for index, flat_ref in enumerate((master, one, two)):
            packed_ref[index, rows, columns] = flat_ref[spot, :]


def weights_kernel(scale_ref, squares_ref, latent_ref, embed_ref, picked_ref, packed_ref):
    factor = total_factor(squares_ref)
    for is_embed, column, rows, columns in packed_slots(latent_ref.shape, embed_ref.shape):
        grad_ref = embed_ref if is_embed else latent_ref
        new_master, _, _ = adam(
            grad_ref[:, column:column + LANES], factor, scale_ref[0], scale_ref[1],
            *(picked_ref[index, rows, columns] for index in range(3)),
        )
        packed_ref[rows, columns] = new_master.astype(packed_ref.dtype)


def state_kernel(core_ref, scale_ref, squares_ref, latent_mine, latent_other, embed_mine, embed_other,
                 master_hbm, one_hbm, two_hbm, average_hbm,
                 master_out, one_out, two_out, average_out,
                 gradient, master_ref, one_ref, two_ref, average_ref, sems):
    load(
        (master_hbm, one_hbm, two_hbm, average_hbm), (master_ref, one_ref, two_ref, average_ref), sems
    )
    core = core_ref[0]
    first_row = 0
    for mine, other in ((latent_mine, latent_other), (embed_mine, embed_other)):
        rows, half = mine.shape
        blocks = half // LANES
        for ref, side in ((mine, core), (other, 1 - core)):
            for block in range(blocks):
                spot = pl.ds(first_row + side * blocks + block, rows, stride=2 * blocks)
                gradient[spot, :] = ref[:, block * LANES:(block + 1) * LANES]
        first_row += rows * 2 * blocks
    new_master, new_one, new_two = adam(
        gradient[...], total_factor(squares_ref), scale_ref[0], scale_ref[1],
        master_ref[...], one_ref[...], two_ref[...],
    )
    master_out[...] = new_master
    one_out[...] = new_one
    two_out[...] = new_two
    average_out[...] = AVG_DECAY * average_ref[...] + (1.0 - AVG_DECAY) * new_master


def assemble_kernel(latent_rows, embed_rows, place_ref, *refs):
    *pieces, latent_out, embed_out = refs
    left_is_mine = place_ref[0] == 0
    width = pieces[0].shape[1]
    stretches = (pieces[0].shape[0] - latent_rows) // embed_rows
    for step in range(len(pieces) // 2):
        owner = place_ref[1] ^ step
        latent_spot = pl.ds(pl.multiple_of(owner * latent_rows, latent_rows), latent_rows)
        embed_spot = pl.ds(pl.multiple_of(owner * embed_rows, embed_rows), embed_rows)
        mine, other = pieces[2 * step], pieces[2 * step + 1]

        def put(out_ref, spot, column, rows):
            half = out_ref.shape[1] // 2
            left = jnp.where(left_is_mine, mine[rows, :], other[rows, :])
            right = jnp.where(left_is_mine, other[rows, :], mine[rows, :])
            out_ref[spot, column:column + width] = left
            out_ref[spot, half + column:half + column + width] = right

        put(latent_out, latent_spot, 0, slice(0, latent_rows))
        for stretch in range(stretches):
            row = latent_rows + stretch * embed_rows
            put(embed_out, embed_spot, stretch * width, slice(row, row + embed_rows))


def direct_shards(kv_up_grads, tok_grads, token_rows, step_count, master, moment_one, moment_two, average):
    n_dp = lax.axis_size("dp")
    core, me = lax.axis_index("group"), lax.axis_index("dp")
    swap = [(0, 1), (1, 0)]

    def half_of(array, side):
        half = array.shape[1] // 2
        return lax.dynamic_slice(array, (0, side * half), (array.shape[0], half))

    latent_got = lax.ppermute(kv_up_grads, "group", swap)
    rows_got = lax.ppermute(token_rows, "group", swap)
    tok_got = lax.ppermute(half_of(tok_grads, 1 - core), "group", swap)

    latent_rows = kv_up_grads.shape[0] // n_dp
    half = kv_up_grads.shape[1] // 2

    def latent_block(owner):
        take = lambda array: lax.dynamic_slice(array, (owner * latent_rows, core * half), (latent_rows, half))
        return take(kv_up_grads).astype(jnp.float32) + take(latent_got).astype(jnp.float32)

    steps = [step for step in (2, 3, 1) if step < n_dp]
    states = [array.reshape(-1, LANES) for array in (master, moment_one, moment_two, average)]

    def send(block, step):
        return lax.ppermute(block, "dp", [(i, i ^ step) for i in range(n_dp)])

    def summed(own, got, scale):
        got = [block.astype(jnp.float32) for block in got]
        return own + sum(got[1:], got[0]) * (1.0 / scale)

    def squares_of(array):
        tile = (array * array).reshape(-1, SUBLANES, array.shape[1]).sum(axis=0)
        return sum(tile[:, i:i + LANES] for i in range(0, array.shape[1], LANES))

    latent_own = latent_block(me)
    latent_sent = [(latent_block(me ^ step) * LATENT_SCALE).astype(jnp.float16) for step in steps]
    latent_own, latent_sent, token_rows, rows_got = lax.optimization_barrier(
        (latent_own, latent_sent, token_rows, rows_got)
    )
    latent_arrived = [send(block, step) for step, block in zip(steps, latent_sent)]

    embed_pair = embed_partial(token_rows, half_of(tok_grads, core)) + embed_partial(rows_got, tok_got)
    embed_rows = embed_pair.shape[0] // n_dp

    def embed_block(owner):
        return lax.dynamic_slice_in_dim(embed_pair, owner * embed_rows, embed_rows, 0)

    embed_own = embed_block(me)
    embed_sent = [(embed_block(me ^ step) * EMBED_SCALE).astype(jnp.float16) for step in steps]
    embed_arrived = [send(block, step) for step, block in zip(steps, embed_sent)]

    place = jnp.stack([core, me]).astype(jnp.int32)
    smem = pl.BlockSpec(memory_space=pltpu.SMEM)
    vmem = pl.BlockSpec(memory_space=pltpu.VMEM)
    hbm = pl.BlockSpec(memory_space=pltpu.HBM)
    packed_rows = latent_rows + embed_own.size // half
    entries = states[0].size
    place, embed_sent = lax.optimization_barrier((place, embed_sent))
    picked = pl.pallas_call(
        functools.partial(pick_kernel, latent_own.shape, embed_own.shape),
        out_shape=jax.ShapeDtypeStruct((3, packed_rows, half), jnp.float32),
        in_specs=[smem] + [hbm] * 3,
        out_specs=vmem,
        scratch_shapes=[pltpu.VMEM(states[0].shape, jnp.float32)] * 3 + [pltpu.SemaphoreType.DMA((3,))],
        compiler_params=pltpu.CompilerParams(vmem_limit_bytes=8 << 20),
        cost_estimate=pl.CostEstimate(flops=0, bytes_accessed=18 * entries, transcendentals=0),
        name="pick",
    )(place, *states[:3])

    latent_arrived, picked = lax.optimization_barrier((latent_arrived, picked))
    latent_sum = summed(latent_own, latent_arrived, LATENT_SCALE)
    squares = squares_of(latent_sum)
    squares, embed_arrived = lax.optimization_barrier((squares, embed_arrived))
    embed_sum = summed(embed_own, embed_arrived, EMBED_SCALE)
    squares = squares + squares_of(embed_sum)
    everyone = ("group", "dp", "mp")
    n_all = lax.axis_size(everyone)
    squares = lax.all_to_all(jnp.tile(squares, (n_all, 1)), everyone, 0, 0, tiled=True)
    scales = jnp.stack(step_scales(step_count))

    packed = pl.pallas_call(
        weights_kernel,
        out_shape=jax.ShapeDtypeStruct((packed_rows, half), jnp.bfloat16),
        in_specs=[smem] + [vmem] * 4,
        out_specs=vmem,
        compiler_params=pltpu.CompilerParams(vmem_limit_bytes=8 << 20),
        name="weights",
    )(scales, squares, latent_sum, embed_sum, picked)

    latent_other = lax.ppermute(latent_sum, "group", swap)
    embed_other = lax.ppermute(embed_sum, "group", swap)
    gathered = {0: packed, **{step: send(packed, step) for step in steps}}

    new_state = pl.pallas_call(
        state_kernel,
        out_shape=[jax.ShapeDtypeStruct(states[0].shape, jnp.float32)] * 4,
        in_specs=[smem] * 2 + [vmem] * 5 + [hbm] * 4,
        out_specs=[vmem] * 4,
        scratch_shapes=[pltpu.VMEM(states[0].shape, jnp.float32)] * 5 + [pltpu.SemaphoreType.DMA((4,))],
        compiler_params=pltpu.CompilerParams(vmem_limit_bytes=16 << 20),
        cost_estimate=pl.CostEstimate(flops=30 * entries, bytes_accessed=36 * entries, transcendentals=2 * entries),
        name="state",
    )(place, scales, squares, latent_sum, latent_other, embed_sum, embed_other, *states)
    pieces = []
    for step in range(n_dp):
        if step:
            gathered[step], new_state = lax.optimization_barrier((gathered[step], new_state))
        pieces += [gathered[step], lax.ppermute(gathered[step], "group", swap)]
    new_kv_up, new_embed = pl.pallas_call(
        functools.partial(assemble_kernel, latent_rows, embed_rows),
        out_shape=[
            jax.ShapeDtypeStruct(kv_up_grads.shape, jnp.bfloat16),
            jax.ShapeDtypeStruct((n_dp * embed_rows, tok_grads.shape[1]), jnp.bfloat16),
        ],
        in_specs=[smem] + [vmem] * len(pieces),
        out_specs=[vmem] * 2,
        compiler_params=pltpu.CompilerParams(vmem_limit_bytes=8 << 20),
        name="assemble",
    )(place, *pieces)
    return (new_kv_up, new_embed, *[array.reshape(master.shape) for array in new_state])


def scattered_shards(kv_up_grads, tok_grads, token_rows, step_count, master, moment_one, moment_two, average):
    latent_part = kv_up_grads.astype(jnp.float32)
    embed_part = embed_partial(token_rows, tok_grads)
    latent_rows, embed_rows = (
        lax.psum_scatter(latent_part, "dp", scatter_dimension=0, tiled=True),
        lax.psum_scatter(embed_part, "dp", scatter_dimension=0, tiled=True),
    )
    latent_rows, embed_rows = lax.psum((latent_rows, embed_rows), "group")
    gradient = jnp.concatenate([latent_rows.reshape(1, -1), embed_rows.reshape(1, -1)], axis=1)
    sum_squares = lax.psum(jnp.sum(gradient * gradient), ("dp", "mp"))
    new_master, new_one, new_two = adam(
        gradient, clip_factor(sum_squares), *step_scales(step_count), master, moment_one, moment_two
    )
    new_average = AVG_DECAY * average + (1.0 - AVG_DECAY) * new_master
    weights = new_master.astype(jnp.bfloat16)
    latent_len = latent_rows.shape[0] * latent_rows.shape[1]
    latent_new = weights[0, :latent_len].reshape(latent_rows.shape)
    embed_new = weights[0, latent_len:].reshape(embed_rows.shape)
    new_kv_up, new_embed = (
        lax.all_gather(latent_new, "dp", axis=0, tiled=True),
        lax.all_gather(embed_new, "dp", axis=0, tiled=True),
    )
    return (new_kv_up, new_embed, new_master, new_one, new_two, new_average)


def solution(mesh):
    placed = (
        P(("group", "dp"), "mp"),
        P(("group", "dp"), None),
        P(("group", "dp")),
        P(),
        P("mp", "dp"),
        P("mp", "dp"),
        P("mp", "dp"),
        P("mp", "dp"),
    )
    few = mesh.shape["group"] == 2 and mesh.shape["dp"] in (2, 4)
    return jax.shard_map(
        direct_shards if few else scattered_shards,
        mesh=mesh,
        in_specs=placed,
        out_specs=(
            P(None, "mp"),
            P("mp", None),
            P("mp", "dp"),
            P("mp", "dp"),
            P("mp", "dp"),
            P("mp", "dp"),
        ),
        check_vma=False,
    )
```

```python
import functools

import jax
import jax.numpy as jnp
from jax import lax
from jax.experimental import pallas as pl
from jax.experimental.pallas import tpu as pltpu
from jax.sharding import PartitionSpec as P

EROWS = 512


BETA_ONE = 0.9
BETA_TWO = 0.95
LEARN_RATE = 0.02
DECAY_RATE = 0.1
EPSILON = 1e-08
CLIP_NORM = 1.0
AVG_DECAY = 0.9

SUBLANES = 8
LANES = 128
STATE_PARTS = 2
STATE_VMEM = 57 << 20
LATENT_SCALE = 256.0
EMBED_SCALE = 8.0


def embed_partial(token_rows, tok_grads):
    block_rows = EROWS // lax.axis_size("mp")
    slot_ids = lax.axis_index("mp") * block_rows + lax.iota(jnp.int32, block_rows)
    onehot = (slot_ids[:, None] == token_rows[None, :]).astype(jnp.bfloat16)
    return jnp.dot(onehot, tok_grads, preferred_element_type=jnp.float32)


def step_scales(step_count):
    step_float = step_count[0].astype(jnp.float32)
    first_scale = 1.0 / (1.0 - jnp.power(jnp.float32(BETA_ONE), step_float))
    second_scale = 1.0 / (1.0 - jnp.power(jnp.float32(BETA_TWO), step_float))
    return first_scale, second_scale


def clip_factor(sum_squares):
    return CLIP_NORM / jnp.maximum(jnp.sqrt(sum_squares), CLIP_NORM)


def adam(gradient, factor, first_scale, second_scale, master, moment_one, moment_two):
    clipped = factor * gradient
    new_one = BETA_ONE * moment_one + (1.0 - BETA_ONE) * clipped
    new_two = BETA_TWO * moment_two + (1.0 - BETA_TWO) * clipped * clipped
    step = (new_one * first_scale) / (jnp.sqrt(new_two * second_scale) + EPSILON)
    new_master = master - LEARN_RATE * (step + DECAY_RATE * master)
    return new_master, new_one, new_two


def total_factor(squares_ref):
    squares = jnp.sum(squares_ref[...], axis=0, keepdims=True)
    return clip_factor(jnp.sum(squares, axis=1, keepdims=True))


def packed_slots(latent_shape, embed_shape):
    latent_rows, width = latent_shape
    embed_rows, embed_half = embed_shape
    for column in range(0, width, LANES):
        yield False, column, slice(0, latent_rows), slice(column, column + LANES)
    for column in range(0, embed_half, LANES):
        row = latent_rows + column // width * embed_rows
        yield True, column, slice(row, row + embed_rows), slice(column % width, column % width + LANES)


def state_spot(shapes, is_embed, column, side):
    height, half = shapes[is_embed]
    start = shapes[0][0] * 2 * shapes[0][1] // LANES if is_embed else 0
    return pl.ds(start + side * (half // LANES) + column // LANES, height, stride=2 * half // LANES)


def load(sources, targets, sems):
    copies = [pltpu.make_async_copy(*pair, sems.at[i]) for i, pair in enumerate(zip(sources, targets))]
    for copy in copies:
        copy.start()
    for copy in copies:
        copy.wait()


def pick_kernel(shapes, place_ref, master_ref, one_ref, two_ref, packed_ref, master, one, two, sems):
    load((master_ref, one_ref, two_ref), (master, one, two), sems)
    for is_embed, column, rows, columns in packed_slots(*shapes):
        spot = state_spot(shapes, is_embed, column, place_ref[0])
        for index, flat_ref in enumerate((master, one, two)):
            packed_ref[index, rows, columns] = flat_ref[spot, :]


def line_steps(me):
    at_end = (me == 0) | (me == 3)
    return jnp.where(at_end, 2, 1), jnp.where(at_end, 1, 2)


def pair_kernel(shapes, place_ref, rows_mine, rows_other, latent_mine, latent_other, tok_mine, tok_other,
                own_ref, sent_ref, embed):
    (latent_rows, half), (embed_rows, embed_half) = shapes
    core, me = place_ref[0], place_ref[1]
    latent_columns = pl.ds(pl.multiple_of(core * half, half), half)
    slots = embed.shape[0]
    slot_ids = lax.broadcasted_iota(jnp.int32, (slots, rows_mine.shape[1]), 0)
    onehots = [(rows[...] == slot_ids).astype(jnp.bfloat16) for rows in (rows_mine, rows_other)]
    columns = pl.ds(pl.multiple_of(core * embed_half, embed_half), embed_half)
    embed[...] = jnp.dot(onehots[0], tok_mine[:, columns], preferred_element_type=jnp.float32) + jnp.dot(
        onehots[1], tok_other[...], preferred_element_type=jnp.float32
    )
    first, second = line_steps(me)
    for index, step in enumerate((0, 3, first, second)):
        out_ref = sent_ref.at[index - 1] if index else own_ref
        latent_scale, embed_scale = (LATENT_SCALE, EMBED_SCALE) if index else (1.0, 1.0)
        owner = me ^ step
        spot = pl.ds(pl.multiple_of(owner * latent_rows, latent_rows), latent_rows)
        pair = latent_mine[spot, :].astype(jnp.float32) + latent_other[spot, latent_columns].astype(jnp.float32)
        out_ref[0:latent_rows, :] = pair * latent_scale
        spot = pl.ds(pl.multiple_of(owner * embed_rows, embed_rows), embed_rows)
        for column in range(0, embed_half, half):
            row = latent_rows + column // half * embed_rows
            out_ref[row:row + embed_rows, :] = embed[spot, column:column + half] * embed_scale


def weights_kernel(scale_ref, squares_ref, grad_ref, picked_ref, packed_ref):
    new_master, _, _ = adam(
        grad_ref[...], total_factor(squares_ref), scale_ref[0], scale_ref[1],
        picked_ref[0], picked_ref[1], picked_ref[2],
    )
    packed_ref[...] = new_master.astype(packed_ref.dtype)


def state_kernel(shapes, place_ref, scale_ref, squares_ref, grad_mine, grad_other, *refs):
    sources, targets, (gradient, inside, outside, in_sems, out_sems) = refs[:4], refs[4:8], refs[8:]
    rows = gradient.shape[0] // STATE_PARTS

    def copies(part):
        spot = pl.ds(part * rows, rows)
        return (
            [pltpu.make_async_copy(ref.at[spot], inside.at[i, spot], in_sems.at[part, i]) for i, ref in enumerate(sources)],
            [pltpu.make_async_copy(outside.at[i, spot], ref.at[spot], out_sems.at[part, i]) for i, ref in enumerate(targets)],
        )

    parts = [copies(part) for part in range(STATE_PARTS)]
    for loads, _ in parts:
        for copy in loads:
            copy.start()
    core = place_ref[0]
    for is_embed, column, packed_rows, columns in packed_slots(*shapes):
        for ref, side in ((grad_mine, core), (grad_other, 1 - core)):
            gradient[state_spot(shapes, is_embed, column, side), :] = ref[packed_rows, columns]
    factor = total_factor(squares_ref)
    for part, (loads, stores) in enumerate(parts):
        for copy in loads:
            copy.wait()
        spot = pl.ds(part * rows, rows)
        new_master, new_one, new_two = adam(
            gradient[spot, :], factor, scale_ref[0], scale_ref[1], inside[0, spot], inside[1, spot], inside[2, spot]
        )
        outside[0, spot] = new_master
        outside[1, spot] = new_one
        outside[2, spot] = new_two
        outside[3, spot] = AVG_DECAY * inside[3, spot] + (1.0 - AVG_DECAY) * new_master
        for copy in stores:
            copy.start()
    for _, stores in parts:
        for copy in stores:
            copy.wait()


def assemble_kernel(latent_rows, embed_rows, place_ref, *refs):
    *pieces, latent_out, embed_out = refs
    left_is_mine = place_ref[0] == 0
    width = pieces[0].shape[1]
    stretches = (pieces[0].shape[0] - latent_rows) // embed_rows
    second, first = line_steps(place_ref[1])
    for index, step in enumerate((0, first, second, 3)):
        owner = place_ref[1] ^ step
        latent_spot = pl.ds(pl.multiple_of(owner * latent_rows, latent_rows), latent_rows)
        embed_spot = pl.ds(pl.multiple_of(owner * embed_rows, embed_rows), embed_rows)
        mine, other = pieces[2 * index], pieces[2 * index + 1]

        def put(out_ref, spot, column, rows):
            half = out_ref.shape[1] // 2
            left = jnp.where(left_is_mine, mine[rows, :], other[rows, :])
            right = jnp.where(left_is_mine, other[rows, :], mine[rows, :])
            out_ref[spot, column:column + width] = left
            out_ref[spot, half + column:half + column + width] = right

        put(latent_out, latent_spot, 0, slice(0, latent_rows))
        for stretch in range(stretches):
            row = latent_rows + stretch * embed_rows
            put(embed_out, embed_spot, stretch * width, slice(row, row + embed_rows))


def direct_shards(kv_up_grads, tok_grads, token_rows, step_count, master, moment_one, moment_two, average):
    n_dp = lax.axis_size("dp")
    core, me = lax.axis_index("group"), lax.axis_index("dp")
    swap = [(0, 1), (1, 0)]

    def half_of(array, side):
        half = array.shape[1] // 2
        return lax.dynamic_slice(array, (0, side * half), (array.shape[0], half))

    latent_got = lax.ppermute(kv_up_grads, "group", swap)
    rows_got = lax.ppermute(token_rows, "group", swap)
    tok_got = lax.ppermute(half_of(tok_grads, 1 - core), "group", swap)

    block_rows = EROWS // lax.axis_size("mp")
    shapes = ((kv_up_grads.shape[0] // n_dp, kv_up_grads.shape[1] // 2), (block_rows // n_dp, tok_grads.shape[1] // 2))
    (latent_rows, half), (embed_rows, embed_half) = shapes
    packed_rows = latent_rows + embed_rows * embed_half // half
    states = [array.reshape(-1, LANES) for array in (master, moment_one, moment_two, average)]
    entries = states[0].size
    place = jnp.stack([core, me]).astype(jnp.int32)

    def slots_of(rows):
        return rows.reshape(1, -1) - lax.axis_index("mp") * block_rows

    smem = pl.BlockSpec(memory_space=pltpu.SMEM)
    vmem = pl.BlockSpec(memory_space=pltpu.VMEM)
    hbm = pl.BlockSpec(memory_space=pltpu.HBM)

    own, sent = pl.pallas_call(
        functools.partial(pair_kernel, shapes),
        out_shape=[
            jax.ShapeDtypeStruct((packed_rows, half), jnp.float32),
            jax.ShapeDtypeStruct((n_dp - 1, packed_rows, half), jnp.float32),
        ],
        in_specs=[smem] + [vmem] * 6,
        out_specs=[vmem] * 2,
        scratch_shapes=[pltpu.VMEM((block_rows, embed_half), jnp.float32)],
        compiler_params=pltpu.CompilerParams(vmem_limit_bytes=12 << 20),
        name="pair",
    )(place, slots_of(token_rows), slots_of(rows_got), half_of(kv_up_grads, core), latent_got, tok_grads, tok_got)
    across, early, late = (sent[index].astype(jnp.float16) for index in range(n_dp - 1))

    inward, middle, first, second = (
        ((0, 1), (3, 2)), ((1, 2), (2, 1)), ((0, 2), (3, 1), (1, 0), (2, 3)), ((0, 1), (3, 2), (1, 3), (2, 0))
    )

    def send(block, pairs):
        return lax.ppermute(block, "dp", pairs)

    across, early = lax.optimization_barrier((across, early))
    passed = send(across, inward)
    from_middle = send(across, middle)
    from_first = send(early, first)
    late = (sent[2] + passed.astype(jnp.float32)).astype(jnp.float16)
    from_second = send(late, second)

    picked_place, late = lax.optimization_barrier((place, late))
    picked = pl.pallas_call(
        functools.partial(pick_kernel, shapes),
        out_shape=jax.ShapeDtypeStruct((3, packed_rows, half), jnp.float32),
        in_specs=[smem] + [hbm] * 3,
        out_specs=vmem,
        scratch_shapes=[pltpu.VMEM(states[0].shape, jnp.float32)] * 3 + [pltpu.SemaphoreType.DMA((3,))],
        compiler_params=pltpu.CompilerParams(vmem_limit_bytes=8 << 20),
        cost_estimate=pl.CostEstimate(flops=0, bytes_accessed=18 * entries, transcendentals=0),
        name="pick",
    )(picked_place, *states[:3])

    from_first, picked = lax.optimization_barrier((from_first, picked))
    is_latent = lax.broadcasted_iota(jnp.int32, (packed_rows, 1), 0) < latent_rows
    unscale = jnp.where(is_latent, 1.0 / LATENT_SCALE, 1.0 / EMBED_SCALE)
    gradient = own + (from_middle.astype(jnp.float32) + from_first.astype(jnp.float32)) * unscale
    from_second, gradient = lax.optimization_barrier((from_second, gradient))
    gradient = gradient + from_second.astype(jnp.float32) * unscale
    squares = (gradient * gradient).reshape(-1, SUBLANES, half).sum(axis=0)
    squares = sum(squares[:, i:i + LANES] for i in range(0, half, LANES))
    everyone = ("group", "dp", "mp")
    n_all = lax.axis_size(everyone)
    squares = lax.all_to_all(jnp.tile(squares, (n_all, 1)), everyone, 0, 0, tiled=True)
    scales = jnp.stack(step_scales(step_count))

    packed = pl.pallas_call(
        weights_kernel,
        out_shape=jax.ShapeDtypeStruct((packed_rows, half), jnp.bfloat16),
        in_specs=[smem] + [vmem] * 3,
        out_specs=vmem,
        compiler_params=pltpu.CompilerParams(vmem_limit_bytes=8 << 20),
        name="weights",
    )(scales, squares, gradient, picked)

    gradient_other = lax.ppermute(gradient, "group", swap)
    from_first = send(packed, first)
    from_second = send(packed, second)
    from_middle = send(packed, middle)
    passed = send(from_first, ((1, 0), (2, 3)))

    state_shape = jax.ShapeDtypeStruct(states[0].shape, jnp.float32)
    new_state = pl.pallas_call(
        functools.partial(state_kernel, shapes),
        out_shape=[state_shape] * 4,
        in_specs=[smem] * 2 + [vmem] * 3 + [hbm] * 4,
        out_specs=[hbm] * 4,
        scratch_shapes=[
            pltpu.VMEM(states[0].shape, jnp.float32),
            pltpu.VMEM((4, *states[0].shape), jnp.float32),
            pltpu.VMEM((4, *states[0].shape), jnp.float32),
            pltpu.SemaphoreType.DMA((STATE_PARTS, 4)),
            pltpu.SemaphoreType.DMA((STATE_PARTS, 4)),
        ],
        compiler_params=pltpu.CompilerParams(vmem_limit_bytes=STATE_VMEM),
        cost_estimate=pl.CostEstimate(flops=30 * entries, bytes_accessed=36 * entries, transcendentals=2 * entries),
        name="state",
    )(place, scales, squares, gradient, gradient_other, *states)
    from_first, new_state = lax.optimization_barrier((from_first, new_state))
    from_second, new_state = lax.optimization_barrier((from_second, new_state))
    inner = (me == 1) | (me == 2)
    gathered = (packed, from_first, from_second, jnp.where(inner, from_middle, passed))
    pieces = []
    for piece in gathered:
        pieces += [piece, lax.ppermute(piece, "group", swap)]
    new_kv_up, new_embed = pl.pallas_call(
        functools.partial(assemble_kernel, latent_rows, embed_rows),
        out_shape=[
            jax.ShapeDtypeStruct(kv_up_grads.shape, jnp.bfloat16),
            jax.ShapeDtypeStruct((n_dp * embed_rows, tok_grads.shape[1]), jnp.bfloat16),
        ],
        in_specs=[smem] + [vmem] * len(pieces),
        out_specs=[vmem] * 2,
        compiler_params=pltpu.CompilerParams(vmem_limit_bytes=8 << 20),
        name="assemble",
    )(place, *pieces)
    return (new_kv_up, new_embed, *[array.reshape(master.shape) for array in new_state])


def scattered_shards(kv_up_grads, tok_grads, token_rows, step_count, master, moment_one, moment_two, average):
    latent_part = kv_up_grads.astype(jnp.float32)
    embed_part = embed_partial(token_rows, tok_grads)
    latent_rows, embed_rows = (
        lax.psum_scatter(latent_part, "dp", scatter_dimension=0, tiled=True),
        lax.psum_scatter(embed_part, "dp", scatter_dimension=0, tiled=True),
    )
    latent_rows, embed_rows = lax.psum((latent_rows, embed_rows), "group")
    gradient = jnp.concatenate([latent_rows.reshape(1, -1), embed_rows.reshape(1, -1)], axis=1)
    sum_squares = lax.psum(jnp.sum(gradient * gradient), ("dp", "mp"))
    new_master, new_one, new_two = adam(
        gradient, clip_factor(sum_squares), *step_scales(step_count), master, moment_one, moment_two
    )
    new_average = AVG_DECAY * average + (1.0 - AVG_DECAY) * new_master
    weights = new_master.astype(jnp.bfloat16)
    latent_len = latent_rows.shape[0] * latent_rows.shape[1]
    latent_new = weights[0, :latent_len].reshape(latent_rows.shape)
    embed_new = weights[0, latent_len:].reshape(embed_rows.shape)
    new_kv_up, new_embed = (
        lax.all_gather(latent_new, "dp", axis=0, tiled=True),
        lax.all_gather(embed_new, "dp", axis=0, tiled=True),
    )
    return (new_kv_up, new_embed, new_master, new_one, new_two, new_average)


def solution(mesh):
    placed = (
        P(("group", "dp"), "mp"),
        P(("group", "dp"), None),
        P(("group", "dp")),
        P(),
        P("mp", "dp"),
        P("mp", "dp"),
        P("mp", "dp"),
        P("mp", "dp"),
    )
    in_line = mesh.shape["group"] == 2 and mesh.shape["dp"] == 4
    return jax.shard_map(
        direct_shards if in_line else scattered_shards,
        mesh=mesh,
        in_specs=placed,
        out_specs=(
            P(None, "mp"),
            P("mp", None),
            P("mp", "dp"),
            P("mp", "dp"),
            P("mp", "dp"),
            P("mp", "dp"),
        ),
        check_vma=False,
    )
```

```python
import functools

import jax
import jax.numpy as jnp
from jax import lax
from jax.experimental import pallas as pl
from jax.experimental.pallas import tpu as pltpu
from jax.sharding import PartitionSpec as P

EROWS = 512


BETA_ONE = 0.9
BETA_TWO = 0.95
LEARN_RATE = 0.02
DECAY_RATE = 0.1
EPSILON = 1e-08
CLIP_NORM = 1.0
AVG_DECAY = 0.9

SUBLANES = 8
LANES = 128
STATE_PARTS = 1
STATE_VMEM = 32 << 20
LATENT_SCALE = 256.0
EMBED_SCALE = 8.0


def embed_partial(token_rows, tok_grads):
    block_rows = EROWS // lax.axis_size("mp")
    slot_ids = lax.axis_index("mp") * block_rows + lax.iota(jnp.int32, block_rows)
    onehot = (slot_ids[:, None] == token_rows[None, :]).astype(jnp.bfloat16)
    return jnp.dot(onehot, tok_grads, preferred_element_type=jnp.float32)


def step_scales(step_count):
    step_float = step_count[0].astype(jnp.float32)
    first_scale = 1.0 / (1.0 - jnp.power(jnp.float32(BETA_ONE), step_float))
    second_scale = 1.0 / (1.0 - jnp.power(jnp.float32(BETA_TWO), step_float))
    return first_scale, second_scale


def clip_factor(sum_squares):
    return CLIP_NORM / jnp.maximum(jnp.sqrt(sum_squares), CLIP_NORM)


def adam(gradient, factor, first_scale, second_scale, master, moment_one, moment_two):
    clipped = factor * gradient
    new_one = BETA_ONE * moment_one + (1.0 - BETA_ONE) * clipped
    new_two = BETA_TWO * moment_two + (1.0 - BETA_TWO) * clipped * clipped
    step = (new_one * first_scale) / (jnp.sqrt(new_two * second_scale) + EPSILON)
    new_master = master - LEARN_RATE * (step + DECAY_RATE * master)
    return new_master, new_one, new_two


def total_factor(squares_ref):
    squares = jnp.sum(squares_ref[...], axis=0, keepdims=True)
    return clip_factor(jnp.sum(squares, axis=1, keepdims=True))


def packed_slots(latent_shape, embed_shape):
    latent_rows, width = latent_shape
    embed_rows, embed_half = embed_shape
    for column in range(0, width, LANES):
        yield False, column, slice(0, latent_rows), slice(column, column + LANES)
    for column in range(0, embed_half, LANES):
        row = latent_rows + column // width * embed_rows
        yield True, column, slice(row, row + embed_rows), slice(column % width, column % width + LANES)


def state_spot(shapes, is_embed, column, side):
    height, half = shapes[is_embed]
    start = shapes[0][0] * 2 * shapes[0][1] // LANES if is_embed else 0
    return pl.ds(start + side * (half // LANES) + column // LANES, height, stride=2 * half // LANES)


def load(sources, targets, sems):
    copies = [pltpu.make_async_copy(*pair, sems.at[i]) for i, pair in enumerate(zip(sources, targets))]
    for copy in copies:
        copy.start()
    for copy in copies:
        copy.wait()


def pick_kernel(shapes, place_ref, master_ref, one_ref, two_ref, packed_ref, master, one, two, sems):
    load((master_ref, one_ref, two_ref), (master, one, two), sems)
    for is_embed, column, rows, columns in packed_slots(*shapes):
        spot = state_spot(shapes, is_embed, column, place_ref[0])
        for index, flat_ref in enumerate((master, one, two)):
            packed_ref[index, rows, columns] = flat_ref[spot, :]


def line_steps(me):
    at_end = (me == 0) | (me == 3)
    return jnp.where(at_end, 2, 1), jnp.where(at_end, 1, 2)


def pair_kernel(shapes, place_ref, rows_mine, rows_other, latent_mine, latent_other, tok_mine, tok_other,
                own_ref, sent_ref, embed):
    (latent_rows, half), (embed_rows, embed_half) = shapes
    core, me = place_ref[0], place_ref[1]
    latent_columns = pl.ds(pl.multiple_of(core * half, half), half)
    slots = embed.shape[0]
    slot_ids = lax.broadcasted_iota(jnp.int32, (slots, rows_mine.shape[1]), 0)
    onehots = [(rows[...] == slot_ids).astype(jnp.bfloat16) for rows in (rows_mine, rows_other)]
    columns = pl.ds(pl.multiple_of(core * embed_half, embed_half), embed_half)
    embed[...] = jnp.dot(onehots[0], tok_mine[:, columns], preferred_element_type=jnp.float32) + jnp.dot(
        onehots[1], tok_other[...], preferred_element_type=jnp.float32
    )
    first, second = line_steps(me)
    for index, step in enumerate((0, 3, first, second)):
        out_ref = sent_ref.at[index - 1] if index else own_ref
        latent_scale, embed_scale = (LATENT_SCALE, EMBED_SCALE) if index else (1.0, 1.0)
        owner = me ^ step
        spot = pl.ds(pl.multiple_of(owner * latent_rows, latent_rows), latent_rows)
        pair = latent_mine[spot, :].astype(jnp.float32) + latent_other[spot, latent_columns].astype(jnp.float32)
        out_ref[0:latent_rows, :] = pair * latent_scale
        spot = pl.ds(pl.multiple_of(owner * embed_rows, embed_rows), embed_rows)
        for column in range(0, embed_half, half):
            row = latent_rows + column // half * embed_rows
            out_ref[row:row + embed_rows, :] = embed[spot, column:column + half] * embed_scale


def weights_kernel(scale_ref, squares_ref, grad_ref, picked_ref, packed_ref):
    new_master, _, _ = adam(
        grad_ref[...], total_factor(squares_ref), scale_ref[0], scale_ref[1],
        picked_ref[0], picked_ref[1], picked_ref[2],
    )
    packed_ref[...] = new_master.astype(packed_ref.dtype)


def state_kernel(shapes, place_ref, scale_ref, squares_ref, grad_mine, grad_other, *refs):
    sources, targets, (gradient, inside, outside, in_sems, out_sems) = refs[:4], refs[4:8], refs[8:]
    rows = gradient.shape[0] // STATE_PARTS

    def copies(part):
        spot = pl.ds(part * rows, rows)
        return (
            [pltpu.make_async_copy(ref.at[spot], inside.at[i, spot], in_sems.at[part, i]) for i, ref in enumerate(sources)],
            [pltpu.make_async_copy(outside.at[i, spot], ref.at[spot], out_sems.at[part, i]) for i, ref in enumerate(targets)],
        )

    parts = [copies(part) for part in range(STATE_PARTS)]
    for loads, _ in parts:
        for copy in loads:
            copy.start()
    core = place_ref[0]
    for is_embed, column, packed_rows, columns in packed_slots(*shapes):
        for ref, side in ((grad_mine, core), (grad_other, 1 - core)):
            gradient[state_spot(shapes, is_embed, column, side), :] = ref[packed_rows, columns]
    factor = total_factor(squares_ref)
    for part, (loads, stores) in enumerate(parts):
        for copy in loads:
            copy.wait()
        spot = pl.ds(part * rows, rows)
        new_master, new_one, new_two = adam(
            gradient[spot, :], factor, scale_ref[0], scale_ref[1], inside[0, spot], inside[1, spot], inside[2, spot]
        )
        outside[0, spot] = new_master
        outside[1, spot] = new_one
        outside[2, spot] = new_two
        outside[3, spot] = AVG_DECAY * inside[3, spot] + (1.0 - AVG_DECAY) * new_master
        for copy in stores:
            copy.start()
    for _, stores in parts:
        for copy in stores:
            copy.wait()


def assemble_kernel(latent_rows, embed_rows, place_ref, *refs):
    *pieces, latent_out, embed_out = refs
    left_is_mine = place_ref[0] == 0
    width = pieces[0].shape[1]
    stretches = (pieces[0].shape[0] - latent_rows) // embed_rows
    second, first = line_steps(place_ref[1])
    for index, step in enumerate((0, first, second, 3)):
        owner = place_ref[1] ^ step
        latent_spot = pl.ds(pl.multiple_of(owner * latent_rows, latent_rows), latent_rows)
        embed_spot = pl.ds(pl.multiple_of(owner * embed_rows, embed_rows), embed_rows)
        mine, other = pieces[2 * index], pieces[2 * index + 1]

        def put(out_ref, spot, column, rows):
            half = out_ref.shape[1] // 2
            left = jnp.where(left_is_mine, mine[rows, :], other[rows, :])
            right = jnp.where(left_is_mine, other[rows, :], mine[rows, :])
            out_ref[spot, column:column + width] = left
            out_ref[spot, half + column:half + column + width] = right

        put(latent_out, latent_spot, 0, slice(0, latent_rows))
        for stretch in range(stretches):
            row = latent_rows + stretch * embed_rows
            put(embed_out, embed_spot, stretch * width, slice(row, row + embed_rows))


def direct_shards(kv_up_grads, tok_grads, token_rows, step_count, master, moment_one, moment_two, average):
    n_dp = lax.axis_size("dp")
    core, me = lax.axis_index("group"), lax.axis_index("dp")
    swap = [(0, 1), (1, 0)]

    def half_of(array, side):
        half = array.shape[1] // 2
        return lax.dynamic_slice(array, (0, side * half), (array.shape[0], half))

    latent_got = lax.ppermute(kv_up_grads, "group", swap)
    rows_got = lax.ppermute(token_rows, "group", swap)
    tok_got = lax.ppermute(half_of(tok_grads, 1 - core), "group", swap)

    block_rows = EROWS // lax.axis_size("mp")
    shapes = ((kv_up_grads.shape[0] // n_dp, kv_up_grads.shape[1] // 2), (block_rows // n_dp, tok_grads.shape[1] // 2))
    (latent_rows, half), (embed_rows, embed_half) = shapes
    packed_rows = latent_rows + embed_rows * embed_half // half
    states = [array.reshape(-1, LANES) for array in (master, moment_one, moment_two, average)]
    entries = states[0].size
    place = jnp.stack([core, me]).astype(jnp.int32)

    def slots_of(rows):
        return rows.reshape(1, -1) - lax.axis_index("mp") * block_rows

    smem = pl.BlockSpec(memory_space=pltpu.SMEM)
    vmem = pl.BlockSpec(memory_space=pltpu.VMEM)
    hbm = pl.BlockSpec(memory_space=pltpu.HBM)

    own, sent = pl.pallas_call(
        functools.partial(pair_kernel, shapes),
        out_shape=[
            jax.ShapeDtypeStruct((packed_rows, half), jnp.float32),
            jax.ShapeDtypeStruct((n_dp - 1, packed_rows, half), jnp.float32),
        ],
        in_specs=[smem] + [vmem] * 6,
        out_specs=[vmem] * 2,
        scratch_shapes=[pltpu.VMEM((block_rows, embed_half), jnp.float32)],
        compiler_params=pltpu.CompilerParams(vmem_limit_bytes=12 << 20),
        name="pair",
    )(place, slots_of(token_rows), slots_of(rows_got), half_of(kv_up_grads, core), latent_got, tok_grads, tok_got)
    across, early, late = (sent[index].astype(jnp.float16) for index in range(n_dp - 1))

    inward, middle, first, second = (
        ((0, 1), (3, 2)), ((1, 2), (2, 1)), ((0, 2), (3, 1), (1, 0), (2, 3)), ((0, 1), (3, 2), (1, 3), (2, 0))
    )

    def send(block, pairs):
        return lax.ppermute(block, "dp", pairs)

    across, early = lax.optimization_barrier((across, early))
    passed = send(across, inward)
    from_middle = send(across, middle)
    from_first = send(early, first)
    late = (sent[2] + passed.astype(jnp.float32)).astype(jnp.float16)
    from_second = send(late, second)

    picked_place, late = lax.optimization_barrier((place, late))
    picked = pl.pallas_call(
        functools.partial(pick_kernel, shapes),
        out_shape=jax.ShapeDtypeStruct((3, packed_rows, half), jnp.float32),
        in_specs=[smem] + [hbm] * 3,
        out_specs=vmem,
        scratch_shapes=[pltpu.VMEM(states[0].shape, jnp.float32)] * 3 + [pltpu.SemaphoreType.DMA((3,))],
        compiler_params=pltpu.CompilerParams(vmem_limit_bytes=8 << 20),
        cost_estimate=pl.CostEstimate(flops=0, bytes_accessed=18 * entries, transcendentals=0),
        name="pick",
    )(picked_place, *states[:3])

    from_first, picked = lax.optimization_barrier((from_first, picked))
    is_latent = lax.broadcasted_iota(jnp.int32, (packed_rows, 1), 0) < latent_rows
    unscale = jnp.where(is_latent, 1.0 / LATENT_SCALE, 1.0 / EMBED_SCALE)
    gradient = own + (from_middle.astype(jnp.float32) + from_first.astype(jnp.float32)) * unscale
    from_second, gradient = lax.optimization_barrier((from_second, gradient))
    gradient = gradient + from_second.astype(jnp.float32) * unscale
    squares = (gradient * gradient).reshape(-1, SUBLANES, half).sum(axis=0)
    squares = sum(squares[:, i:i + LANES] for i in range(0, half, LANES))
    everyone = ("group", "dp", "mp")
    n_all = lax.axis_size(everyone)
    squares = lax.all_to_all(jnp.tile(squares, (n_all, 1)), everyone, 0, 0, tiled=True)
    scales = jnp.stack(step_scales(step_count))

    packed = pl.pallas_call(
        weights_kernel,
        out_shape=jax.ShapeDtypeStruct((packed_rows, half), jnp.bfloat16),
        in_specs=[smem] + [vmem] * 3,
        out_specs=vmem,
        compiler_params=pltpu.CompilerParams(vmem_limit_bytes=8 << 20),
        name="weights",
    )(scales, squares, gradient, picked)

    gradient_other = lax.ppermute(gradient, "group", swap)
    from_first = send(packed, first)
    from_second = send(packed, second)

    state_shape = jax.ShapeDtypeStruct(states[0].shape, jnp.float32)
    new_state = pl.pallas_call(
        functools.partial(state_kernel, shapes),
        out_shape=[state_shape] * 4,
        in_specs=[smem] * 2 + [vmem] * 3 + [hbm] * 4,
        out_specs=[hbm] * 4,
        scratch_shapes=[
            pltpu.VMEM(states[0].shape, jnp.float32),
            pltpu.VMEM((4, *states[0].shape), jnp.float32),
            pltpu.VMEM((4, *states[0].shape), jnp.float32),
            pltpu.SemaphoreType.DMA((STATE_PARTS, 4)),
            pltpu.SemaphoreType.DMA((STATE_PARTS, 4)),
        ],
        compiler_params=pltpu.CompilerParams(vmem_limit_bytes=STATE_VMEM),
        cost_estimate=pl.CostEstimate(flops=30 * entries, bytes_accessed=36 * entries, transcendentals=2 * entries),
        name="state",
    )(place, scales, squares, gradient, gradient_other, *states)
    packed, new_state = lax.optimization_barrier((packed, new_state))
    from_middle = send(packed, middle)
    from_first, new_state = lax.optimization_barrier((from_first, new_state))
    passed = send(from_first, ((1, 0), (2, 3)))
    inner = (me == 1) | (me == 2)
    gathered = (packed, from_first, from_second, jnp.where(inner, from_middle, passed))
    pieces = []
    for piece in gathered:
        pieces += [piece, lax.ppermute(piece, "group", swap)]
    new_kv_up, new_embed = pl.pallas_call(
        functools.partial(assemble_kernel, latent_rows, embed_rows),
        out_shape=[
            jax.ShapeDtypeStruct(kv_up_grads.shape, jnp.bfloat16),
            jax.ShapeDtypeStruct((n_dp * embed_rows, tok_grads.shape[1]), jnp.bfloat16),
        ],
        in_specs=[smem] + [vmem] * len(pieces),
        out_specs=[vmem] * 2,
        compiler_params=pltpu.CompilerParams(vmem_limit_bytes=8 << 20),
        name="assemble",
    )(place, *pieces)
    return (new_kv_up, new_embed, *[array.reshape(master.shape) for array in new_state])


def scattered_shards(kv_up_grads, tok_grads, token_rows, step_count, master, moment_one, moment_two, average):
    latent_part = kv_up_grads.astype(jnp.float32)
    embed_part = embed_partial(token_rows, tok_grads)
    latent_rows, embed_rows = (
        lax.psum_scatter(latent_part, "dp", scatter_dimension=0, tiled=True),
        lax.psum_scatter(embed_part, "dp", scatter_dimension=0, tiled=True),
    )
    latent_rows, embed_rows = lax.psum((latent_rows, embed_rows), "group")
    gradient = jnp.concatenate([latent_rows.reshape(1, -1), embed_rows.reshape(1, -1)], axis=1)
    sum_squares = lax.psum(jnp.sum(gradient * gradient), ("dp", "mp"))
    new_master, new_one, new_two = adam(
        gradient, clip_factor(sum_squares), *step_scales(step_count), master, moment_one, moment_two
    )
    new_average = AVG_DECAY * average + (1.0 - AVG_DECAY) * new_master
    weights = new_master.astype(jnp.bfloat16)
    latent_len = latent_rows.shape[0] * latent_rows.shape[1]
    latent_new = weights[0, :latent_len].reshape(latent_rows.shape)
    embed_new = weights[0, latent_len:].reshape(embed_rows.shape)
    new_kv_up, new_embed = (
        lax.all_gather(latent_new, "dp", axis=0, tiled=True),
        lax.all_gather(embed_new, "dp", axis=0, tiled=True),
    )
    return (new_kv_up, new_embed, new_master, new_one, new_two, new_average)


def solution(mesh):
    placed = (
        P(("group", "dp"), "mp"),
        P(("group", "dp"), None),
        P(("group", "dp")),
        P(),
        P("mp", "dp"),
        P("mp", "dp"),
        P("mp", "dp"),
        P("mp", "dp"),
    )
    in_line = mesh.shape["group"] == 2 and mesh.shape["dp"] == 4
    return jax.shard_map(
        direct_shards if in_line else scattered_shards,
        mesh=mesh,
        in_specs=placed,
        out_specs=(
            P(None, "mp"),
            P("mp", None),
            P("mp", "dp"),
            P("mp", "dp"),
            P("mp", "dp"),
            P("mp", "dp"),
        ),
        check_vma=False,
    )
```

```python
import functools

import jax
import jax.numpy as jnp
from jax import lax
from jax.experimental import pallas as pl
from jax.experimental.pallas import tpu as pltpu
from jax.sharding import PartitionSpec as P

EROWS = 512


BETA_ONE = 0.9
BETA_TWO = 0.95
LEARN_RATE = 0.02
DECAY_RATE = 0.1
EPSILON = 1e-08
CLIP_NORM = 1.0
AVG_DECAY = 0.9

SUBLANES = 8
LANES = 128
STATE_PARTS = 1
STATE_VMEM = 32 << 20
LATENT_SCALE = 256.0
EMBED_SCALE = 8.0


def embed_partial(token_rows, tok_grads):
    block_rows = EROWS // lax.axis_size("mp")
    slot_ids = lax.axis_index("mp") * block_rows + lax.iota(jnp.int32, block_rows)
    onehot = (slot_ids[:, None] == token_rows[None, :]).astype(jnp.bfloat16)
    return jnp.dot(onehot, tok_grads, preferred_element_type=jnp.float32)


def step_scales(step_count):
    step_float = step_count[0].astype(jnp.float32)
    first_scale = 1.0 / (1.0 - jnp.power(jnp.float32(BETA_ONE), step_float))
    second_scale = 1.0 / (1.0 - jnp.power(jnp.float32(BETA_TWO), step_float))
    return first_scale, second_scale


def clip_factor(sum_squares):
    return CLIP_NORM / jnp.maximum(jnp.sqrt(sum_squares), CLIP_NORM)


def adam(gradient, factor, first_scale, second_scale, master, moment_one, moment_two):
    clipped = factor * gradient
    new_one = BETA_ONE * moment_one + (1.0 - BETA_ONE) * clipped
    new_two = BETA_TWO * moment_two + (1.0 - BETA_TWO) * clipped * clipped
    step = (new_one * first_scale) / (jnp.sqrt(new_two * second_scale) + EPSILON)
    new_master = master - LEARN_RATE * (step + DECAY_RATE * master)
    return new_master, new_one, new_two


def total_factor(squares_ref):
    squares = jnp.sum(squares_ref[...], axis=0, keepdims=True)
    return clip_factor(jnp.sum(squares, axis=1, keepdims=True))


def packed_slots(latent_shape, embed_shape):
    latent_rows, width = latent_shape
    embed_rows, embed_half = embed_shape
    for column in range(0, width, LANES):
        yield False, column, slice(0, latent_rows), slice(column, column + LANES)
    for column in range(0, embed_half, LANES):
        row = latent_rows + column // width * embed_rows
        yield True, column, slice(row, row + embed_rows), slice(column % width, column % width + LANES)


def state_spot(shapes, is_embed, column, side):
    height, half = shapes[is_embed]
    start = shapes[0][0] * 2 * shapes[0][1] // LANES if is_embed else 0
    return pl.ds(start + side * (half // LANES) + column // LANES, height, stride=2 * half // LANES)


def load(sources, targets, sems):
    copies = [pltpu.make_async_copy(*pair, sems.at[i]) for i, pair in enumerate(zip(sources, targets))]
    for copy in copies:
        copy.start()
    for copy in copies:
        copy.wait()


def pick_kernel(shapes, place_ref, master_ref, one_ref, two_ref, packed_ref, master, one, two, sems):
    load((master_ref, one_ref, two_ref), (master, one, two), sems)
    for is_embed, column, rows, columns in packed_slots(*shapes):
        spot = state_spot(shapes, is_embed, column, place_ref[0])
        for index, flat_ref in enumerate((master, one, two)):
            packed_ref[index, rows, columns] = flat_ref[spot, :]


def line_steps(me):
    at_end = (me == 0) | (me == 3)
    return jnp.where(at_end, 2, 1), jnp.where(at_end, 1, 2)


def pack_pair(shapes, owner, latent_mine, latent_other, embed, out_ref, latent_scale, embed_scale):
    (latent_rows, half), (embed_rows, embed_half) = shapes
    out_ref[0:latent_rows, :] = (latent_mine.astype(jnp.float32) + latent_other.astype(jnp.float32)) * latent_scale
    spot = pl.ds(pl.multiple_of(owner * embed_rows, embed_rows), embed_rows)
    for column in range(0, embed_half, half):
        row = latent_rows + column // half * embed_rows
        out_ref[row:row + embed_rows, :] = embed[spot, column:column + half] * embed_scale


def across_kernel(shapes, place_ref, rows_mine, rows_other, latent_mine, latent_other, tok_mine, tok_other,
                  across_ref, embed_ref):
    (latent_rows, half), (_, embed_half) = shapes
    core, owner = place_ref[0], place_ref[1] ^ 3
    slots = embed_ref.shape[0]
    ids = place_ref[2] * slots + lax.broadcasted_iota(jnp.int32, (slots, rows_mine.shape[1]), 0)
    onehots = [(rows[...] == ids).astype(jnp.bfloat16) for rows in (rows_mine, rows_other)]
    columns = pl.ds(pl.multiple_of(core * embed_half, embed_half), embed_half)
    embed_ref[...] = jnp.dot(onehots[0], tok_mine[:, columns], preferred_element_type=jnp.float32) + jnp.dot(
        onehots[1], tok_other[...], preferred_element_type=jnp.float32
    )
    spot = pl.ds(pl.multiple_of(owner * latent_rows, latent_rows), latent_rows)
    columns = pl.ds(pl.multiple_of(core * half, half), half)
    pack_pair(
        shapes, owner, latent_mine[...], latent_other[spot, columns], embed_ref, across_ref, LATENT_SCALE, EMBED_SCALE
    )


def rest_kernel(shapes, place_ref, latent_mine, latent_other, embed_ref, own_ref, sent_ref):
    latent_rows, half = shapes[0]
    core, me = place_ref[0], place_ref[1]
    columns = pl.ds(pl.multiple_of(core * half, half), half)
    for index, step in enumerate((0, *line_steps(me))):
        spot = pl.ds(pl.multiple_of((me ^ step) * latent_rows, latent_rows), latent_rows)
        pack_pair(
            shapes, me ^ step, latent_mine[spot, :], latent_other[spot, columns], embed_ref,
            sent_ref.at[index - 1] if index else own_ref,
            LATENT_SCALE if index else 1.0, EMBED_SCALE if index else 1.0,
        )


def weights_kernel(scale_ref, squares_ref, grad_ref, picked_ref, packed_ref):
    new_master, _, _ = adam(
        grad_ref[...], total_factor(squares_ref), scale_ref[0], scale_ref[1],
        picked_ref[0], picked_ref[1], picked_ref[2],
    )
    packed_ref[...] = new_master.astype(packed_ref.dtype)


def state_kernel(shapes, place_ref, scale_ref, squares_ref, grad_mine, grad_other, *refs):
    sources, targets, (gradient, inside, outside, in_sems, out_sems) = refs[:4], refs[4:8], refs[8:]
    rows = gradient.shape[0] // STATE_PARTS

    def copies(part):
        spot = pl.ds(part * rows, rows)
        return (
            [pltpu.make_async_copy(ref.at[spot], inside.at[i, spot], in_sems.at[part, i]) for i, ref in enumerate(sources)],
            [pltpu.make_async_copy(outside.at[i, spot], ref.at[spot], out_sems.at[part, i]) for i, ref in enumerate(targets)],
        )

    parts = [copies(part) for part in range(STATE_PARTS)]
    for loads, _ in parts:
        for copy in loads:
            copy.start()
    core = place_ref[0]
    for is_embed, column, packed_rows, columns in packed_slots(*shapes):
        for ref, side in ((grad_mine, core), (grad_other, 1 - core)):
            gradient[state_spot(shapes, is_embed, column, side), :] = ref[packed_rows, columns]
    factor = total_factor(squares_ref)
    for part, (loads, stores) in enumerate(parts):
        for copy in loads:
            copy.wait()
        spot = pl.ds(part * rows, rows)
        new_master, new_one, new_two = adam(
            gradient[spot, :], factor, scale_ref[0], scale_ref[1], inside[0, spot], inside[1, spot], inside[2, spot]
        )
        outside[0, spot] = new_master
        outside[1, spot] = new_one
        outside[2, spot] = new_two
        outside[3, spot] = AVG_DECAY * inside[3, spot] + (1.0 - AVG_DECAY) * new_master
        for copy in stores:
            copy.start()
    for _, stores in parts:
        for copy in stores:
            copy.wait()


def assemble_kernel(latent_rows, embed_rows, place_ref, *refs):
    *pieces, latent_out, embed_out = refs
    left_is_mine = place_ref[0] == 0
    width = pieces[0].shape[1]
    stretches = (pieces[0].shape[0] - latent_rows) // embed_rows
    second, first = line_steps(place_ref[1])
    for index, step in enumerate((0, first, second, 3)):
        owner = place_ref[1] ^ step
        latent_spot = pl.ds(pl.multiple_of(owner * latent_rows, latent_rows), latent_rows)
        embed_spot = pl.ds(pl.multiple_of(owner * embed_rows, embed_rows), embed_rows)
        mine, other = pieces[2 * index], pieces[2 * index + 1]

        def put(out_ref, spot, column, rows):
            half = out_ref.shape[1] // 2
            left = jnp.where(left_is_mine, mine[rows, :], other[rows, :])
            right = jnp.where(left_is_mine, other[rows, :], mine[rows, :])
            out_ref[spot, column:column + width] = left
            out_ref[spot, half + column:half + column + width] = right

        put(latent_out, latent_spot, 0, slice(0, latent_rows))
        for stretch in range(stretches):
            row = latent_rows + stretch * embed_rows
            put(embed_out, embed_spot, stretch * width, slice(row, row + embed_rows))


def direct_shards(kv_up_grads, tok_grads, token_rows, step_count, master, moment_one, moment_two, average):
    n_dp = lax.axis_size("dp")
    core, me = lax.axis_index("group"), lax.axis_index("dp")
    swap = [(0, 1), (1, 0)]

    def half_of(array, side):
        half = array.shape[1] // 2
        return lax.dynamic_slice(array, (0, side * half), (array.shape[0], half))

    latent_got = lax.ppermute(kv_up_grads, "group", swap)
    rows_got = lax.ppermute(token_rows, "group", swap)
    tok_got = lax.ppermute(half_of(tok_grads, 1 - core), "group", swap)

    block_rows = EROWS // lax.axis_size("mp")
    shapes = ((kv_up_grads.shape[0] // n_dp, kv_up_grads.shape[1] // 2), (block_rows // n_dp, tok_grads.shape[1] // 2))
    (latent_rows, half), (embed_rows, embed_half) = shapes
    packed_rows = latent_rows + embed_rows * embed_half // half
    states = [array.reshape(-1, LANES) for array in (master, moment_one, moment_two, average)]
    entries = states[0].size
    place = jnp.stack([core, me, lax.axis_index("mp")]).astype(jnp.int32)

    smem = pl.BlockSpec(memory_space=pltpu.SMEM)
    vmem = pl.BlockSpec(memory_space=pltpu.VMEM)
    hbm = pl.BlockSpec(memory_space=pltpu.HBM)

    packed_shape = jax.ShapeDtypeStruct((packed_rows, half), jnp.float32)
    across_rows = lax.dynamic_slice(kv_up_grads, ((me ^ 3) * latent_rows, core * half), (latent_rows, half))
    across, embed = pl.pallas_call(
        functools.partial(across_kernel, shapes),
        out_shape=[packed_shape, jax.ShapeDtypeStruct((block_rows, embed_half), jnp.float32)],
        in_specs=[smem] + [vmem] * 6,
        out_specs=[vmem] * 2,
        compiler_params=pltpu.CompilerParams(vmem_limit_bytes=12 << 20),
        name="across",
    )(place, token_rows.reshape(1, -1), rows_got.reshape(1, -1), across_rows, latent_got, tok_grads, tok_got)
    across = across.astype(jnp.float16)
    across, kv_up_grads = lax.optimization_barrier((across, kv_up_grads))
    across_middle, place = lax.optimization_barrier((across, place))
    own, sent = pl.pallas_call(
        functools.partial(rest_kernel, shapes),
        out_shape=[packed_shape, jax.ShapeDtypeStruct((2, packed_rows, half), jnp.float32)],
        in_specs=[smem] + [vmem] * 3,
        out_specs=[vmem] * 2,
        compiler_params=pltpu.CompilerParams(vmem_limit_bytes=12 << 20),
        cost_estimate=pl.CostEstimate(flops=4 * entries, bytes_accessed=16 * entries, transcendentals=0),
        name="rest",
    )(place, half_of(kv_up_grads, core), latent_got, embed)
    early = sent[0].astype(jnp.float16)

    inward, middle, first, second = (
        ((0, 1), (3, 2)), ((1, 2), (2, 1)), ((0, 2), (3, 1), (1, 0), (2, 3)), ((0, 1), (3, 2), (1, 3), (2, 0))
    )

    def send(block, pairs):
        return lax.ppermute(block, "dp", pairs)

    passed = send(across, inward)
    from_middle = send(across_middle, middle)
    from_first = send(early, first)
    late = (sent[1] + passed.astype(jnp.float32)).astype(jnp.float16)
    from_second = send(late, second)

    picked_place, late = lax.optimization_barrier((place, late))
    picked = pl.pallas_call(
        functools.partial(pick_kernel, shapes),
        out_shape=jax.ShapeDtypeStruct((3, packed_rows, half), jnp.float32),
        in_specs=[smem] + [hbm] * 3,
        out_specs=vmem,
        scratch_shapes=[pltpu.VMEM(states[0].shape, jnp.float32)] * 3 + [pltpu.SemaphoreType.DMA((3,))],
        compiler_params=pltpu.CompilerParams(vmem_limit_bytes=8 << 20),
        cost_estimate=pl.CostEstimate(flops=0, bytes_accessed=18 * entries, transcendentals=0),
        name="pick",
    )(picked_place, *states[:3])

    from_first, picked = lax.optimization_barrier((from_first, picked))
    is_latent = lax.broadcasted_iota(jnp.int32, (packed_rows, 1), 0) < latent_rows
    unscale = jnp.where(is_latent, 1.0 / LATENT_SCALE, 1.0 / EMBED_SCALE)
    gradient = own + (from_middle.astype(jnp.float32) + from_first.astype(jnp.float32)) * unscale
    from_second, gradient = lax.optimization_barrier((from_second, gradient))
    gradient = gradient + from_second.astype(jnp.float32) * unscale
    squares = (gradient * gradient).reshape(-1, SUBLANES, half).sum(axis=0)
    squares = sum(squares[:, i:i + LANES] for i in range(0, half, LANES))
    everyone = ("group", "dp", "mp")
    n_all = lax.axis_size(everyone)
    squares = lax.all_to_all(jnp.tile(squares, (n_all, 1)), everyone, 0, 0, tiled=True)
    scales = jnp.stack(step_scales(step_count))

    packed = pl.pallas_call(
        weights_kernel,
        out_shape=jax.ShapeDtypeStruct((packed_rows, half), jnp.bfloat16),
        in_specs=[smem] + [vmem] * 3,
        out_specs=vmem,
        compiler_params=pltpu.CompilerParams(vmem_limit_bytes=8 << 20),
        name="weights",
    )(scales, squares, gradient, picked)

    gradient_other = lax.ppermute(gradient, "group", swap)
    from_first = send(packed, first)
    from_second = send(packed, second)

    state_shape = jax.ShapeDtypeStruct(states[0].shape, jnp.float32)
    new_state = pl.pallas_call(
        functools.partial(state_kernel, shapes),
        out_shape=[state_shape] * 4,
        in_specs=[smem] * 2 + [vmem] * 3 + [hbm] * 4,
        out_specs=[hbm] * 4,
        scratch_shapes=[
            pltpu.VMEM(states[0].shape, jnp.float32),
            pltpu.VMEM((4, *states[0].shape), jnp.float32),
            pltpu.VMEM((4, *states[0].shape), jnp.float32),
            pltpu.SemaphoreType.DMA((STATE_PARTS, 4)),
            pltpu.SemaphoreType.DMA((STATE_PARTS, 4)),
        ],
        compiler_params=pltpu.CompilerParams(vmem_limit_bytes=STATE_VMEM),
        cost_estimate=pl.CostEstimate(flops=30 * entries, bytes_accessed=36 * entries, transcendentals=2 * entries),
        name="state",
    )(place, scales, squares, gradient, gradient_other, *states)
    packed, new_state = lax.optimization_barrier((packed, new_state))
    from_middle = send(packed, middle)
    from_first, new_state = lax.optimization_barrier((from_first, new_state))
    passed = send(from_first, ((1, 0), (2, 3)))
    inner = (me == 1) | (me == 2)
    gathered = (packed, from_first, from_second, jnp.where(inner, from_middle, passed))
    pieces = []
    for piece in gathered:
        pieces += [piece, lax.ppermute(piece, "group", swap)]
    new_kv_up, new_embed = pl.pallas_call(
        functools.partial(assemble_kernel, latent_rows, embed_rows),
        out_shape=[
            jax.ShapeDtypeStruct(kv_up_grads.shape, jnp.bfloat16),
            jax.ShapeDtypeStruct((n_dp * embed_rows, tok_grads.shape[1]), jnp.bfloat16),
        ],
        in_specs=[smem] + [vmem] * len(pieces),
        out_specs=[vmem] * 2,
        compiler_params=pltpu.CompilerParams(vmem_limit_bytes=8 << 20),
        name="assemble",
    )(place, *pieces)
    return (new_kv_up, new_embed, *[array.reshape(master.shape) for array in new_state])


def scattered_shards(kv_up_grads, tok_grads, token_rows, step_count, master, moment_one, moment_two, average):
    latent_part = kv_up_grads.astype(jnp.float32)
    embed_part = embed_partial(token_rows, tok_grads)
    latent_rows, embed_rows = (
        lax.psum_scatter(latent_part, "dp", scatter_dimension=0, tiled=True),
        lax.psum_scatter(embed_part, "dp", scatter_dimension=0, tiled=True),
    )
    latent_rows, embed_rows = lax.psum((latent_rows, embed_rows), "group")
    gradient = jnp.concatenate([latent_rows.reshape(1, -1), embed_rows.reshape(1, -1)], axis=1)
    sum_squares = lax.psum(jnp.sum(gradient * gradient), ("dp", "mp"))
    new_master, new_one, new_two = adam(
        gradient, clip_factor(sum_squares), *step_scales(step_count), master, moment_one, moment_two
    )
    new_average = AVG_DECAY * average + (1.0 - AVG_DECAY) * new_master
    weights = new_master.astype(jnp.bfloat16)
    latent_len = latent_rows.shape[0] * latent_rows.shape[1]
    latent_new = weights[0, :latent_len].reshape(latent_rows.shape)
    embed_new = weights[0, latent_len:].reshape(embed_rows.shape)
    new_kv_up, new_embed = (
        lax.all_gather(latent_new, "dp", axis=0, tiled=True),
        lax.all_gather(embed_new, "dp", axis=0, tiled=True),
    )
    return (new_kv_up, new_embed, new_master, new_one, new_two, new_average)


def solution(mesh):
    placed = (
        P(("group", "dp"), "mp"),
        P(("group", "dp"), None),
        P(("group", "dp")),
        P(),
        P("mp", "dp"),
        P("mp", "dp"),
        P("mp", "dp"),
        P("mp", "dp"),
    )
    in_line = mesh.shape["group"] == 2 and mesh.shape["dp"] == 4
    return jax.shard_map(
        direct_shards if in_line else scattered_shards,
        mesh=mesh,
        in_specs=placed,
        out_specs=(
            P(None, "mp"),
            P("mp", None),
            P("mp", "dp"),
            P("mp", "dp"),
            P("mp", "dp"),
            P("mp", "dp"),
        ),
        check_vma=False,
    )
```

```python
import functools

import jax
import jax.numpy as jnp
from jax import lax
from jax.experimental import pallas as pl
from jax.experimental.pallas import tpu as pltpu
from jax.sharding import PartitionSpec as P

EROWS = 512


BETA_ONE = 0.9
BETA_TWO = 0.95
LEARN_RATE = 0.02
DECAY_RATE = 0.1
EPSILON = 1e-08
CLIP_NORM = 1.0
AVG_DECAY = 0.9

SUBLANES = 8
LANES = 128
STATE_PARTS = 1
STATE_VMEM = 32 << 20
LATENT_SCALE = 256.0
EMBED_SCALE = 8.0


def embed_partial(token_rows, tok_grads):
    block_rows = EROWS // lax.axis_size("mp")
    slot_ids = lax.axis_index("mp") * block_rows + lax.iota(jnp.int32, block_rows)
    onehot = (slot_ids[:, None] == token_rows[None, :]).astype(jnp.bfloat16)
    return jnp.dot(onehot, tok_grads, preferred_element_type=jnp.float32)


def step_scales(step_count):
    step_float = step_count[0].astype(jnp.float32)
    first_scale = 1.0 / (1.0 - jnp.power(jnp.float32(BETA_ONE), step_float))
    second_scale = 1.0 / (1.0 - jnp.power(jnp.float32(BETA_TWO), step_float))
    return first_scale, second_scale


def clip_factor(sum_squares):
    return CLIP_NORM / jnp.maximum(jnp.sqrt(sum_squares), CLIP_NORM)


def adam(gradient, factor, first_scale, second_scale, master, moment_one, moment_two):
    clipped = factor * gradient
    new_one = BETA_ONE * moment_one + (1.0 - BETA_ONE) * clipped
    new_two = BETA_TWO * moment_two + (1.0 - BETA_TWO) * clipped * clipped
    step = (new_one * first_scale) / (jnp.sqrt(new_two * second_scale) + EPSILON)
    new_master = master - LEARN_RATE * (step + DECAY_RATE * master)
    return new_master, new_one, new_two


def total_factor(squares_ref):
    squares = jnp.sum(squares_ref[...], axis=0, keepdims=True)
    return clip_factor(jnp.sum(squares, axis=1, keepdims=True))


def packed_slots(latent_shape, embed_shape):
    latent_rows, width = latent_shape
    embed_rows, embed_half = embed_shape
    for column in range(0, width, LANES):
        yield False, column, slice(0, latent_rows), slice(column, column + LANES)
    for column in range(0, embed_half, LANES):
        row = latent_rows + column // width * embed_rows
        yield True, column, slice(row, row + embed_rows), slice(column % width, column % width + LANES)


def state_spot(shapes, is_embed, column, side):
    height, half = shapes[is_embed]
    start = shapes[0][0] * 2 * shapes[0][1] // LANES if is_embed else 0
    return pl.ds(start + side * (half // LANES) + column // LANES, height, stride=2 * half // LANES)


def load(sources, targets, sems):
    copies = [pltpu.make_async_copy(*pair, sems.at[i]) for i, pair in enumerate(zip(sources, targets))]
    for copy in copies:
        copy.start()
    for copy in copies:
        copy.wait()


def pick_kernel(shapes, place_ref, master_ref, one_ref, two_ref, packed_ref, master, one, two, sems):
    load((master_ref, one_ref, two_ref), (master, one, two), sems)
    for is_embed, column, rows, columns in packed_slots(*shapes):
        spot = state_spot(shapes, is_embed, column, place_ref[0])
        for index, flat_ref in enumerate((master, one, two)):
            packed_ref[index, rows, columns] = flat_ref[spot, :]


def line_steps(me):
    at_end = (me == 0) | (me == 3)
    return jnp.where(at_end, 2, 1), jnp.where(at_end, 1, 2)


def pack_pair(shapes, owner, latent_mine, latent_other, embed, out_ref, latent_scale, embed_scale):
    (latent_rows, half), (embed_rows, embed_half) = shapes
    out_ref[0:latent_rows, :] = (latent_mine.astype(jnp.float32) + latent_other.astype(jnp.float32)) * latent_scale
    spot = pl.ds(pl.multiple_of(owner * embed_rows, embed_rows), embed_rows)
    for column in range(0, embed_half, half):
        row = latent_rows + column // half * embed_rows
        out_ref[row:row + embed_rows, :] = embed[spot, column:column + half] * embed_scale


def across_kernel(shapes, rows_mine, rows_other, latent_mine, latent_other, tok_mine, tok_other,
                  across_ref, embed_ref):
    (latent_rows, half), (_, embed_half) = shapes
    core, owner = lax.axis_index("group"), lax.axis_index("dp") ^ 3
    slots = embed_ref.shape[0]
    ids = lax.axis_index("mp") * slots + lax.broadcasted_iota(jnp.int32, (slots, rows_mine.shape[1]), 0)
    onehots = [(rows[...] == ids).astype(jnp.bfloat16) for rows in (rows_mine, rows_other)]
    columns = pl.ds(pl.multiple_of(core * embed_half, embed_half), embed_half)
    embed_ref[...] = jnp.dot(onehots[0], tok_mine[:, columns], preferred_element_type=jnp.float32) + jnp.dot(
        onehots[1], tok_other[...], preferred_element_type=jnp.float32
    )
    spot = pl.ds(pl.multiple_of(owner * latent_rows, latent_rows), latent_rows)
    columns = pl.ds(pl.multiple_of(core * half, half), half)
    pack_pair(
        shapes, owner, latent_mine[...], latent_other[spot, columns], embed_ref, across_ref, LATENT_SCALE, EMBED_SCALE
    )


def rest_kernel(shapes, latent_mine, latent_other, embed_ref, own_ref, sent_ref):
    latent_rows, half = shapes[0]
    core, me = lax.axis_index("group"), lax.axis_index("dp")
    columns = pl.ds(pl.multiple_of(core * half, half), half)
    for index, step in enumerate((0, *line_steps(me))):
        spot = pl.ds(pl.multiple_of((me ^ step) * latent_rows, latent_rows), latent_rows)
        pack_pair(
            shapes, me ^ step, latent_mine[spot, :], latent_other[spot, columns], embed_ref,
            sent_ref.at[index - 1] if index else own_ref,
            LATENT_SCALE if index else 1.0, EMBED_SCALE if index else 1.0,
        )


def weights_kernel(scale_ref, squares_ref, grad_ref, picked_ref, packed_ref):
    new_master, _, _ = adam(
        grad_ref[...], total_factor(squares_ref), scale_ref[0:1, :], scale_ref[1:2, :],
        picked_ref[0], picked_ref[1], picked_ref[2],
    )
    packed_ref[...] = new_master.astype(packed_ref.dtype)


def state_kernel(shapes, place_ref, scale_ref, squares_ref, grad_mine, grad_other, *refs):
    sources, targets, (gradient, inside, outside, in_sems, out_sems) = refs[:4], refs[4:8], refs[8:]
    rows = gradient.shape[0] // STATE_PARTS

    def copies(part):
        spot = pl.ds(part * rows, rows)
        return (
            [pltpu.make_async_copy(ref.at[spot], inside.at[i, spot], in_sems.at[part, i]) for i, ref in enumerate(sources)],
            [pltpu.make_async_copy(outside.at[i, spot], ref.at[spot], out_sems.at[part, i]) for i, ref in enumerate(targets)],
        )

    parts = [copies(part) for part in range(STATE_PARTS)]
    for loads, _ in parts:
        for copy in loads:
            copy.start()
    core = place_ref[0]
    for is_embed, column, packed_rows, columns in packed_slots(*shapes):
        for ref, side in ((grad_mine, core), (grad_other, 1 - core)):
            gradient[state_spot(shapes, is_embed, column, side), :] = ref[packed_rows, columns]
    factor = total_factor(squares_ref)
    for part, (loads, stores) in enumerate(parts):
        for copy in loads:
            copy.wait()
        spot = pl.ds(part * rows, rows)
        new_master, new_one, new_two = adam(
            gradient[spot, :], factor, scale_ref[0], scale_ref[1], inside[0, spot], inside[1, spot], inside[2, spot]
        )
        outside[0, spot] = new_master
        outside[1, spot] = new_one
        outside[2, spot] = new_two
        outside[3, spot] = AVG_DECAY * inside[3, spot] + (1.0 - AVG_DECAY) * new_master
        for copy in stores:
            copy.start()
    for _, stores in parts:
        for copy in stores:
            copy.wait()


def assemble_kernel(latent_rows, embed_rows, *refs):
    *pieces, latent_out, embed_out = refs
    left_is_mine, me = lax.axis_index("group") == 0, lax.axis_index("dp")
    width = pieces[0].shape[1]
    stretches = (pieces[0].shape[0] - latent_rows) // embed_rows
    second, first = line_steps(me)
    for index, step in enumerate((0, first, second, 3)):
        owner = me ^ step
        latent_spot = pl.ds(pl.multiple_of(owner * latent_rows, latent_rows), latent_rows)
        embed_spot = pl.ds(pl.multiple_of(owner * embed_rows, embed_rows), embed_rows)
        mine, other = pieces[2 * index], pieces[2 * index + 1]

        def put(out_ref, spot, column, rows):
            half = out_ref.shape[1] // 2
            left = jnp.where(left_is_mine, mine[rows, :], other[rows, :])
            right = jnp.where(left_is_mine, other[rows, :], mine[rows, :])
            out_ref[spot, column:column + width] = left
            out_ref[spot, half + column:half + column + width] = right

        put(latent_out, latent_spot, 0, slice(0, latent_rows))
        for stretch in range(stretches):
            row = latent_rows + stretch * embed_rows
            put(embed_out, embed_spot, stretch * width, slice(row, row + embed_rows))


def direct_shards(kv_up_grads, tok_grads, token_rows, step_count, master, moment_one, moment_two, average):
    n_dp = lax.axis_size("dp")
    core, me = lax.axis_index("group"), lax.axis_index("dp")
    swap = [(0, 1), (1, 0)]

    def half_of(array, side):
        half = array.shape[1] // 2
        return lax.dynamic_slice(array, (0, side * half), (array.shape[0], half))

    latent_got = lax.ppermute(kv_up_grads, "group", swap)
    rows_got = lax.ppermute(token_rows, "group", swap)
    tok_got = lax.ppermute(half_of(tok_grads, 1 - core), "group", swap)

    block_rows = EROWS // lax.axis_size("mp")
    shapes = ((kv_up_grads.shape[0] // n_dp, kv_up_grads.shape[1] // 2), (block_rows // n_dp, tok_grads.shape[1] // 2))
    (latent_rows, half), (embed_rows, embed_half) = shapes
    packed_rows = latent_rows + embed_rows * embed_half // half
    states = [array.reshape(-1, LANES) for array in (master, moment_one, moment_two, average)]
    entries = states[0].size
    place = jnp.stack([core, me, lax.axis_index("mp")]).astype(jnp.int32)

    smem = pl.BlockSpec(memory_space=pltpu.SMEM)
    vmem = pl.BlockSpec(memory_space=pltpu.VMEM)
    hbm = pl.BlockSpec(memory_space=pltpu.HBM)

    packed_shape = jax.ShapeDtypeStruct((packed_rows, half), jnp.float32)
    across_rows = lax.dynamic_slice(kv_up_grads, ((me ^ 3) * latent_rows, core * half), (latent_rows, half))
    across, embed = pl.pallas_call(
        functools.partial(across_kernel, shapes),
        out_shape=[packed_shape, jax.ShapeDtypeStruct((block_rows, embed_half), jnp.float32)],
        in_specs=[vmem] * 6,
        out_specs=[vmem] * 2,
        compiler_params=pltpu.CompilerParams(vmem_limit_bytes=12 << 20),
        name="across",
    )(token_rows.reshape(1, -1), rows_got.reshape(1, -1), across_rows, latent_got, tok_grads, tok_got)
    across = across.astype(jnp.float16)
    across, kv_up_grads = lax.optimization_barrier((across, kv_up_grads))
    across_middle, place = lax.optimization_barrier((across, place))
    own, sent = pl.pallas_call(
        functools.partial(rest_kernel, shapes),
        out_shape=[packed_shape, jax.ShapeDtypeStruct((2, packed_rows, half), jnp.float32)],
        in_specs=[vmem] * 3,
        out_specs=[vmem] * 2,
        compiler_params=pltpu.CompilerParams(vmem_limit_bytes=12 << 20),
        cost_estimate=pl.CostEstimate(flops=4 * entries, bytes_accessed=16 * entries, transcendentals=0),
        name="rest",
    )(half_of(kv_up_grads, core), latent_got, embed)
    early = sent[0].astype(jnp.float16)

    inward, middle, first, second = (
        ((0, 1), (3, 2)), ((1, 2), (2, 1)), ((0, 2), (3, 1), (1, 0), (2, 3)), ((0, 1), (3, 2), (1, 3), (2, 0))
    )

    def send(block, pairs):
        return lax.ppermute(block, "dp", pairs)

    passed = send(across, inward)
    from_middle = send(across_middle, middle)
    from_first = send(early, first)
    late = (sent[1] + passed.astype(jnp.float32)).astype(jnp.float16)
    from_second = send(late, second)

    picked_place, late = lax.optimization_barrier((place, late))
    picked = pl.pallas_call(
        functools.partial(pick_kernel, shapes),
        out_shape=jax.ShapeDtypeStruct((3, packed_rows, half), jnp.float32),
        in_specs=[smem] + [hbm] * 3,
        out_specs=vmem,
        scratch_shapes=[pltpu.VMEM(states[0].shape, jnp.float32)] * 3 + [pltpu.SemaphoreType.DMA((3,))],
        compiler_params=pltpu.CompilerParams(vmem_limit_bytes=8 << 20),
        cost_estimate=pl.CostEstimate(flops=0, bytes_accessed=18 * entries, transcendentals=0),
        name="pick",
    )(picked_place, *states[:3])

    from_first, picked = lax.optimization_barrier((from_first, picked))
    is_latent = lax.broadcasted_iota(jnp.int32, (packed_rows, 1), 0) < latent_rows
    unscale = jnp.where(is_latent, 1.0 / LATENT_SCALE, 1.0 / EMBED_SCALE)
    gradient = own + (from_middle.astype(jnp.float32) + from_first.astype(jnp.float32)) * unscale
    from_second, gradient = lax.optimization_barrier((from_second, gradient))
    gradient = gradient + from_second.astype(jnp.float32) * unscale
    squares = (gradient * gradient).reshape(-1, SUBLANES, half).sum(axis=0)
    squares = sum(squares[:, i:i + LANES] for i in range(0, half, LANES))
    everyone = ("group", "dp", "mp")
    n_all = lax.axis_size(everyone)
    squares = lax.all_to_all(jnp.tile(squares, (n_all, 1)), everyone, 0, 0, tiled=True)
    scales = jnp.stack(step_scales(step_count))

    packed = pl.pallas_call(
        weights_kernel,
        out_shape=jax.ShapeDtypeStruct((packed_rows, half), jnp.bfloat16),
        in_specs=[vmem] * 4,
        out_specs=vmem,
        compiler_params=pltpu.CompilerParams(vmem_limit_bytes=8 << 20),
        name="weights",
    )(jnp.broadcast_to(scales[:, None], (2, half)), squares, gradient, picked)

    gradient_other = lax.ppermute(gradient, "group", swap)
    from_first = send(packed, first)
    from_second = send(packed, second)

    state_shape = jax.ShapeDtypeStruct(states[0].shape, jnp.float32)
    new_state = pl.pallas_call(
        functools.partial(state_kernel, shapes),
        out_shape=[state_shape] * 4,
        in_specs=[smem] * 2 + [vmem] * 3 + [hbm] * 4,
        out_specs=[hbm] * 4,
        scratch_shapes=[
            pltpu.VMEM(states[0].shape, jnp.float32),
            pltpu.VMEM((4, *states[0].shape), jnp.float32),
            pltpu.VMEM((4, *states[0].shape), jnp.float32),
            pltpu.SemaphoreType.DMA((STATE_PARTS, 4)),
            pltpu.SemaphoreType.DMA((STATE_PARTS, 4)),
        ],
        compiler_params=pltpu.CompilerParams(vmem_limit_bytes=STATE_VMEM),
        cost_estimate=pl.CostEstimate(flops=30 * entries, bytes_accessed=36 * entries, transcendentals=2 * entries),
        name="state",
    )(place, scales, squares, gradient, gradient_other, *states)
    packed, new_state = lax.optimization_barrier((packed, new_state))
    from_middle = send(packed, middle)
    from_first, new_state = lax.optimization_barrier((from_first, new_state))
    passed = send(from_first, ((1, 0), (2, 3)))
    inner = (me == 1) | (me == 2)
    gathered = (packed, from_first, from_second, jnp.where(inner, from_middle, passed))
    pieces = []
    for piece in gathered:
        pieces += [piece, lax.ppermute(piece, "group", swap)]
    new_kv_up, new_embed = pl.pallas_call(
        functools.partial(assemble_kernel, latent_rows, embed_rows),
        out_shape=[
            jax.ShapeDtypeStruct(kv_up_grads.shape, jnp.bfloat16),
            jax.ShapeDtypeStruct((n_dp * embed_rows, tok_grads.shape[1]), jnp.bfloat16),
        ],
        in_specs=[vmem] * len(pieces),
        out_specs=[vmem] * 2,
        compiler_params=pltpu.CompilerParams(vmem_limit_bytes=8 << 20),
        name="assemble",
    )(*pieces)
    return (new_kv_up, new_embed, *[array.reshape(master.shape) for array in new_state])


def scattered_shards(kv_up_grads, tok_grads, token_rows, step_count, master, moment_one, moment_two, average):
    latent_part = kv_up_grads.astype(jnp.float32)
    embed_part = embed_partial(token_rows, tok_grads)
    latent_rows, embed_rows = (
        lax.psum_scatter(latent_part, "dp", scatter_dimension=0, tiled=True),
        lax.psum_scatter(embed_part, "dp", scatter_dimension=0, tiled=True),
    )
    latent_rows, embed_rows = lax.psum((latent_rows, embed_rows), "group")
    gradient = jnp.concatenate([latent_rows.reshape(1, -1), embed_rows.reshape(1, -1)], axis=1)
    sum_squares = lax.psum(jnp.sum(gradient * gradient), ("dp", "mp"))
    new_master, new_one, new_two = adam(
        gradient, clip_factor(sum_squares), *step_scales(step_count), master, moment_one, moment_two
    )
    new_average = AVG_DECAY * average + (1.0 - AVG_DECAY) * new_master
    weights = new_master.astype(jnp.bfloat16)
    latent_len = latent_rows.shape[0] * latent_rows.shape[1]
    latent_new = weights[0, :latent_len].reshape(latent_rows.shape)
    embed_new = weights[0, latent_len:].reshape(embed_rows.shape)
    new_kv_up, new_embed = (
        lax.all_gather(latent_new, "dp", axis=0, tiled=True),
        lax.all_gather(embed_new, "dp", axis=0, tiled=True),
    )
    return (new_kv_up, new_embed, new_master, new_one, new_two, new_average)


def solution(mesh):
    placed = (
        P(("group", "dp"), "mp"),
        P(("group", "dp"), None),
        P(("group", "dp")),
        P(),
        P("mp", "dp"),
        P("mp", "dp"),
        P("mp", "dp"),
        P("mp", "dp"),
    )
    in_line = mesh.shape["group"] == 2 and mesh.shape["dp"] == 4
    return jax.shard_map(
        direct_shards if in_line else scattered_shards,
        mesh=mesh,
        in_specs=placed,
        out_specs=(
            P(None, "mp"),
            P("mp", None),
            P("mp", "dp"),
            P("mp", "dp"),
            P("mp", "dp"),
            P("mp", "dp"),
        ),
        check_vma=False,
    )
```

```python
import functools

import jax
import jax.numpy as jnp
from jax import lax
from jax.experimental import pallas as pl
from jax.experimental.pallas import tpu as pltpu
from jax.sharding import PartitionSpec as P

EROWS = 512


BETA_ONE = 0.9
BETA_TWO = 0.95
LEARN_RATE = 0.02
DECAY_RATE = 0.1
EPSILON = 1e-08
CLIP_NORM = 1.0
AVG_DECAY = 0.9

SUBLANES = 8
LANES = 128
STATE_PARTS = 1
STATE_VMEM = 32 << 20
LATENT_SCALE = 256.0
EMBED_SCALE = 8.0


def embed_partial(token_rows, tok_grads):
    block_rows = EROWS // lax.axis_size("mp")
    slot_ids = lax.axis_index("mp") * block_rows + lax.iota(jnp.int32, block_rows)
    onehot = (slot_ids[:, None] == token_rows[None, :]).astype(jnp.bfloat16)
    return jnp.dot(onehot, tok_grads, preferred_element_type=jnp.float32)


def step_scales(step_count):
    step_float = step_count[0].astype(jnp.float32)
    first_scale = 1.0 / (1.0 - jnp.power(jnp.float32(BETA_ONE), step_float))
    second_scale = 1.0 / (1.0 - jnp.power(jnp.float32(BETA_TWO), step_float))
    return first_scale, second_scale


def clip_factor(sum_squares):
    return CLIP_NORM / jnp.maximum(jnp.sqrt(sum_squares), CLIP_NORM)


def adam(gradient, factor, first_scale, second_scale, master, moment_one, moment_two):
    clipped = factor * gradient
    new_one = BETA_ONE * moment_one + (1.0 - BETA_ONE) * clipped
    new_two = BETA_TWO * moment_two + (1.0 - BETA_TWO) * clipped * clipped
    step = (new_one * first_scale) / (jnp.sqrt(new_two * second_scale) + EPSILON)
    new_master = master - LEARN_RATE * (step + DECAY_RATE * master)
    return new_master, new_one, new_two


def total_factor(squares_ref):
    squares = jnp.sum(squares_ref[...], axis=0, keepdims=True)
    return clip_factor(jnp.sum(squares, axis=1, keepdims=True))


def packed_slots(latent_shape, embed_shape):
    latent_rows, width = latent_shape
    embed_rows, embed_half = embed_shape
    for column in range(0, width, LANES):
        yield False, column, slice(0, latent_rows), slice(column, column + LANES)
    for column in range(0, embed_half, LANES):
        row = latent_rows + column // width * embed_rows
        yield True, column, slice(row, row + embed_rows), slice(column % width, column % width + LANES)


def state_spot(shapes, is_embed, column, side):
    height, half = shapes[is_embed]
    start = shapes[0][0] * 2 * shapes[0][1] // LANES if is_embed else 0
    return pl.ds(start + side * (half // LANES) + column // LANES, height, stride=2 * half // LANES)


def load(sources, targets, sems):
    copies = [pltpu.make_async_copy(*pair, sems.at[i]) for i, pair in enumerate(zip(sources, targets))]
    for copy in copies:
        copy.start()
    for copy in copies:
        copy.wait()


def pick_kernel(shapes, place_ref, master_ref, one_ref, two_ref, packed_ref, master, one, two, sems):
    load((master_ref, one_ref, two_ref), (master, one, two), sems)
    for is_embed, column, rows, columns in packed_slots(*shapes):
        spot = state_spot(shapes, is_embed, column, place_ref[0])
        for index, flat_ref in enumerate((master, one, two)):
            packed_ref[index, rows, columns] = flat_ref[spot, :]


def line_steps(me):
    at_end = (me == 0) | (me == 3)
    return jnp.where(at_end, 2, 1), jnp.where(at_end, 1, 2)


def pack_pair(shapes, owner, latent_mine, latent_other, embed, out_ref, latent_scale, embed_scale):
    (latent_rows, half), (embed_rows, embed_half) = shapes
    out_ref[0:latent_rows, :] = (latent_mine.astype(jnp.float32) + latent_other.astype(jnp.float32)) * latent_scale
    spot = pl.ds(pl.multiple_of(owner * embed_rows, embed_rows), embed_rows)
    for column in range(0, embed_half, half):
        row = latent_rows + column // half * embed_rows
        out_ref[row:row + embed_rows, :] = embed[spot, column:column + half] * embed_scale


def onehot_kernel(rows_ref, onehot_ref):
    slots, tokens = onehot_ref.shape
    ids = lax.axis_index("mp") * slots + lax.broadcasted_iota(jnp.int32, (slots, tokens), 0)
    onehot_ref[...] = (rows_ref[...] == ids).astype(onehot_ref.dtype)


def across_kernel(shapes, rows_mine, onehot_other, latent_mine, latent_other, tok_mine, tok_other,
                  across_ref, embed_ref):
    (latent_rows, half), (_, embed_half) = shapes
    core, owner = lax.axis_index("group"), lax.axis_index("dp") ^ 3
    slots = embed_ref.shape[0]
    ids = lax.axis_index("mp") * slots + lax.broadcasted_iota(jnp.int32, (slots, rows_mine.shape[1]), 0)
    onehots = [(rows_mine[...] == ids).astype(jnp.bfloat16), onehot_other[...]]
    columns = pl.ds(pl.multiple_of(core * embed_half, embed_half), embed_half)
    embed_ref[...] = jnp.dot(onehots[0], tok_mine[:, columns], preferred_element_type=jnp.float32) + jnp.dot(
        onehots[1], tok_other[...], preferred_element_type=jnp.float32
    )
    spot = pl.ds(pl.multiple_of(owner * latent_rows, latent_rows), latent_rows)
    columns = pl.ds(pl.multiple_of(core * half, half), half)
    pack_pair(
        shapes, owner, latent_mine[...], latent_other[spot, columns], embed_ref, across_ref, LATENT_SCALE, EMBED_SCALE
    )


def rest_kernel(shapes, latent_mine, latent_other, embed_ref, own_ref, sent_ref):
    latent_rows, half = shapes[0]
    core, me = lax.axis_index("group"), lax.axis_index("dp")
    columns = pl.ds(pl.multiple_of(core * half, half), half)
    for index, step in enumerate((0, *line_steps(me))):
        spot = pl.ds(pl.multiple_of((me ^ step) * latent_rows, latent_rows), latent_rows)
        pack_pair(
            shapes, me ^ step, latent_mine[spot, :], latent_other[spot, columns], embed_ref,
            sent_ref.at[index - 1] if index else own_ref,
            LATENT_SCALE if index else 1.0, EMBED_SCALE if index else 1.0,
        )


def weights_kernel(scale_ref, squares_ref, grad_ref, picked_ref, packed_ref):
    new_master, _, _ = adam(
        grad_ref[...], total_factor(squares_ref), scale_ref[0:1, :], scale_ref[1:2, :],
        picked_ref[0], picked_ref[1], picked_ref[2],
    )
    packed_ref[...] = new_master.astype(packed_ref.dtype)


def state_kernel(shapes, place_ref, scale_ref, squares_ref, grad_mine, grad_other, *refs):
    sources, targets, (gradient, inside, outside, in_sems, out_sems) = refs[:4], refs[4:8], refs[8:]
    rows = gradient.shape[0] // STATE_PARTS

    def copies(part):
        spot = pl.ds(part * rows, rows)
        return (
            [pltpu.make_async_copy(ref.at[spot], inside.at[i, spot], in_sems.at[part, i]) for i, ref in enumerate(sources)],
            [pltpu.make_async_copy(outside.at[i, spot], ref.at[spot], out_sems.at[part, i]) for i, ref in enumerate(targets)],
        )

    parts = [copies(part) for part in range(STATE_PARTS)]
    for loads, _ in parts:
        for copy in loads:
            copy.start()
    core = place_ref[0]
    for is_embed, column, packed_rows, columns in packed_slots(*shapes):
        for ref, side in ((grad_mine, core), (grad_other, 1 - core)):
            gradient[state_spot(shapes, is_embed, column, side), :] = ref[packed_rows, columns]
    factor = total_factor(squares_ref)
    for part, (loads, stores) in enumerate(parts):
        for copy in loads:
            copy.wait()
        spot = pl.ds(part * rows, rows)
        new_master, new_one, new_two = adam(
            gradient[spot, :], factor, scale_ref[0], scale_ref[1], inside[0, spot], inside[1, spot], inside[2, spot]
        )
        outside[0, spot] = new_master
        outside[1, spot] = new_one
        outside[2, spot] = new_two
        outside[3, spot] = AVG_DECAY * inside[3, spot] + (1.0 - AVG_DECAY) * new_master
        for copy in stores:
            copy.start()
    for _, stores in parts:
        for copy in stores:
            copy.wait()


def assemble_kernel(latent_rows, embed_rows, *refs):
    *pieces, latent_out, embed_out = refs
    left_is_mine, me = lax.axis_index("group") == 0, lax.axis_index("dp")
    width = pieces[0].shape[1]
    stretches = (pieces[0].shape[0] - latent_rows) // embed_rows
    second, first = line_steps(me)
    for index, step in enumerate((0, first, second, 3)):
        owner = me ^ step
        latent_spot = pl.ds(pl.multiple_of(owner * latent_rows, latent_rows), latent_rows)
        embed_spot = pl.ds(pl.multiple_of(owner * embed_rows, embed_rows), embed_rows)
        mine, other = pieces[2 * index], pieces[2 * index + 1]

        def put(out_ref, spot, column, rows):
            half = out_ref.shape[1] // 2
            left = jnp.where(left_is_mine, mine[rows, :], other[rows, :])
            right = jnp.where(left_is_mine, other[rows, :], mine[rows, :])
            out_ref[spot, column:column + width] = left
            out_ref[spot, half + column:half + column + width] = right

        put(latent_out, latent_spot, 0, slice(0, latent_rows))
        for stretch in range(stretches):
            row = latent_rows + stretch * embed_rows
            put(embed_out, embed_spot, stretch * width, slice(row, row + embed_rows))


def direct_shards(kv_up_grads, tok_grads, token_rows, step_count, master, moment_one, moment_two, average):
    n_dp = lax.axis_size("dp")
    core, me = lax.axis_index("group"), lax.axis_index("dp")
    swap = [(0, 1), (1, 0)]

    def half_of(array, side):
        half = array.shape[1] // 2
        return lax.dynamic_slice(array, (0, side * half), (array.shape[0], half))

    latent_got = lax.ppermute(kv_up_grads, "group", swap)
    rows_got = lax.ppermute(token_rows, "group", swap)
    tok_got = lax.ppermute(half_of(tok_grads, 1 - core), "group", swap)

    block_rows = EROWS // lax.axis_size("mp")
    shapes = ((kv_up_grads.shape[0] // n_dp, kv_up_grads.shape[1] // 2), (block_rows // n_dp, tok_grads.shape[1] // 2))
    (latent_rows, half), (embed_rows, embed_half) = shapes
    packed_rows = latent_rows + embed_rows * embed_half // half
    states = [array.reshape(-1, LANES) for array in (master, moment_one, moment_two, average)]
    entries = states[0].size
    place = jnp.stack([core, me, lax.axis_index("mp")]).astype(jnp.int32)

    smem = pl.BlockSpec(memory_space=pltpu.SMEM)
    vmem = pl.BlockSpec(memory_space=pltpu.VMEM)
    hbm = pl.BlockSpec(memory_space=pltpu.HBM)

    packed_shape = jax.ShapeDtypeStruct((packed_rows, half), jnp.float32)
    onehot_other = pl.pallas_call(
        onehot_kernel,
        out_shape=jax.ShapeDtypeStruct((block_rows, token_rows.size), jnp.bfloat16),
        in_specs=[vmem],
        out_specs=vmem,
        cost_estimate=pl.CostEstimate(flops=0, bytes_accessed=1 << 23, transcendentals=0),
        compiler_params=pltpu.CompilerParams(vmem_limit_bytes=4 << 20),
        name="onehot",
    )(rows_got.reshape(1, -1))
    across_rows = lax.dynamic_slice(kv_up_grads, ((me ^ 3) * latent_rows, core * half), (latent_rows, half))
    across, embed = pl.pallas_call(
        functools.partial(across_kernel, shapes),
        out_shape=[packed_shape, jax.ShapeDtypeStruct((block_rows, embed_half), jnp.float32)],
        in_specs=[vmem] * 6,
        out_specs=[vmem] * 2,
        compiler_params=pltpu.CompilerParams(vmem_limit_bytes=12 << 20),
        name="across",
    )(token_rows.reshape(1, -1), onehot_other, across_rows, latent_got, tok_grads, tok_got)
    across = across.astype(jnp.float16)
    across, kv_up_grads = lax.optimization_barrier((across, kv_up_grads))
    across_middle, place = lax.optimization_barrier((across, place))
    own, sent = pl.pallas_call(
        functools.partial(rest_kernel, shapes),
        out_shape=[packed_shape, jax.ShapeDtypeStruct((2, packed_rows, half), jnp.float32)],
        in_specs=[vmem] * 3,
        out_specs=[vmem] * 2,
        compiler_params=pltpu.CompilerParams(vmem_limit_bytes=12 << 20),
        cost_estimate=pl.CostEstimate(flops=4 * entries, bytes_accessed=16 * entries, transcendentals=0),
        name="rest",
    )(half_of(kv_up_grads, core), latent_got, embed)
    early = sent[0].astype(jnp.float16)

    inward, middle, first, second = (
        ((0, 1), (3, 2)), ((1, 2), (2, 1)), ((0, 2), (3, 1), (1, 0), (2, 3)), ((0, 1), (3, 2), (1, 3), (2, 0))
    )

    def send(block, pairs):
        return lax.ppermute(block, "dp", pairs)

    passed = send(across, inward)
    from_middle = send(across_middle, middle)
    from_first = send(early, first)
    late = (sent[1] + passed.astype(jnp.float32)).astype(jnp.float16)
    from_second = send(late, second)

    picked_place, late = lax.optimization_barrier((place, late))
    picked = pl.pallas_call(
        functools.partial(pick_kernel, shapes),
        out_shape=jax.ShapeDtypeStruct((3, packed_rows, half), jnp.float32),
        in_specs=[smem] + [hbm] * 3,
        out_specs=vmem,
        scratch_shapes=[pltpu.VMEM(states[0].shape, jnp.float32)] * 3 + [pltpu.SemaphoreType.DMA((3,))],
        compiler_params=pltpu.CompilerParams(vmem_limit_bytes=8 << 20),
        cost_estimate=pl.CostEstimate(flops=0, bytes_accessed=18 * entries, transcendentals=0),
        name="pick",
    )(picked_place, *states[:3])

    from_first, picked = lax.optimization_barrier((from_first, picked))
    is_latent = lax.broadcasted_iota(jnp.int32, (packed_rows, 1), 0) < latent_rows
    unscale = jnp.where(is_latent, 1.0 / LATENT_SCALE, 1.0 / EMBED_SCALE)
    gradient = own + (from_middle.astype(jnp.float32) + from_first.astype(jnp.float32)) * unscale
    from_second, gradient = lax.optimization_barrier((from_second, gradient))
    gradient = gradient + from_second.astype(jnp.float32) * unscale
    squares = (gradient * gradient).reshape(-1, SUBLANES, half).sum(axis=0)
    squares = sum(squares[:, i:i + LANES] for i in range(0, half, LANES))
    everyone = ("group", "dp", "mp")
    n_all = lax.axis_size(everyone)
    squares = lax.all_to_all(jnp.tile(squares, (n_all, 1)), everyone, 0, 0, tiled=True)
    scales = jnp.stack(step_scales(step_count))

    packed = pl.pallas_call(
        weights_kernel,
        out_shape=jax.ShapeDtypeStruct((packed_rows, half), jnp.bfloat16),
        in_specs=[vmem] * 4,
        out_specs=vmem,
        compiler_params=pltpu.CompilerParams(vmem_limit_bytes=8 << 20),
        name="weights",
    )(jnp.broadcast_to(scales[:, None], (2, half)), squares, gradient, picked)

    gradient_other = lax.ppermute(gradient, "group", swap)
    from_first = send(packed, first)
    from_second = send(packed, second)

    state_shape = jax.ShapeDtypeStruct(states[0].shape, jnp.float32)
    new_state = pl.pallas_call(
        functools.partial(state_kernel, shapes),
        out_shape=[state_shape] * 4,
        in_specs=[smem] * 2 + [vmem] * 3 + [hbm] * 4,
        out_specs=[hbm] * 4,
        scratch_shapes=[
            pltpu.VMEM(states[0].shape, jnp.float32),
            pltpu.VMEM((4, *states[0].shape), jnp.float32),
            pltpu.VMEM((4, *states[0].shape), jnp.float32),
            pltpu.SemaphoreType.DMA((STATE_PARTS, 4)),
            pltpu.SemaphoreType.DMA((STATE_PARTS, 4)),
        ],
        compiler_params=pltpu.CompilerParams(vmem_limit_bytes=STATE_VMEM),
        cost_estimate=pl.CostEstimate(flops=30 * entries, bytes_accessed=36 * entries, transcendentals=2 * entries),
        name="state",
    )(place, scales, squares, gradient, gradient_other, *states)
    packed, new_state = lax.optimization_barrier((packed, new_state))
    from_middle = send(packed, middle)
    from_first, new_state = lax.optimization_barrier((from_first, new_state))
    passed = send(from_first, ((1, 0), (2, 3)))
    inner = (me == 1) | (me == 2)
    gathered = (packed, from_first, from_second, jnp.where(inner, from_middle, passed))
    pieces = []
    for piece in gathered:
        pieces += [piece, lax.ppermute(piece, "group", swap)]
    new_kv_up, new_embed = pl.pallas_call(
        functools.partial(assemble_kernel, latent_rows, embed_rows),
        out_shape=[
            jax.ShapeDtypeStruct(kv_up_grads.shape, jnp.bfloat16),
            jax.ShapeDtypeStruct((n_dp * embed_rows, tok_grads.shape[1]), jnp.bfloat16),
        ],
        in_specs=[vmem] * len(pieces),
        out_specs=[vmem] * 2,
        compiler_params=pltpu.CompilerParams(vmem_limit_bytes=8 << 20),
        name="assemble",
    )(*pieces)
    return (new_kv_up, new_embed, *[array.reshape(master.shape) for array in new_state])


def scattered_shards(kv_up_grads, tok_grads, token_rows, step_count, master, moment_one, moment_two, average):
    latent_part = kv_up_grads.astype(jnp.float32)
    embed_part = embed_partial(token_rows, tok_grads)
    latent_rows, embed_rows = (
        lax.psum_scatter(latent_part, "dp", scatter_dimension=0, tiled=True),
        lax.psum_scatter(embed_part, "dp", scatter_dimension=0, tiled=True),
    )
    latent_rows, embed_rows = lax.psum((latent_rows, embed_rows), "group")
    gradient = jnp.concatenate([latent_rows.reshape(1, -1), embed_rows.reshape(1, -1)], axis=1)
    sum_squares = lax.psum(jnp.sum(gradient * gradient), ("dp", "mp"))
    new_master, new_one, new_two = adam(
        gradient, clip_factor(sum_squares), *step_scales(step_count), master, moment_one, moment_two
    )
    new_average = AVG_DECAY * average + (1.0 - AVG_DECAY) * new_master
    weights = new_master.astype(jnp.bfloat16)
    latent_len = latent_rows.shape[0] * latent_rows.shape[1]
    latent_new = weights[0, :latent_len].reshape(latent_rows.shape)
    embed_new = weights[0, latent_len:].reshape(embed_rows.shape)
    new_kv_up, new_embed = (
        lax.all_gather(latent_new, "dp", axis=0, tiled=True),
        lax.all_gather(embed_new, "dp", axis=0, tiled=True),
    )
    return (new_kv_up, new_embed, new_master, new_one, new_two, new_average)


def solution(mesh):
    placed = (
        P(("group", "dp"), "mp"),
        P(("group", "dp"), None),
        P(("group", "dp")),
        P(),
        P("mp", "dp"),
        P("mp", "dp"),
        P("mp", "dp"),
        P("mp", "dp"),
    )
    in_line = mesh.shape["group"] == 2 and mesh.shape["dp"] == 4
    return jax.shard_map(
        direct_shards if in_line else scattered_shards,
        mesh=mesh,
        in_specs=placed,
        out_specs=(
            P(None, "mp"),
            P("mp", None),
            P("mp", "dp"),
            P("mp", "dp"),
            P("mp", "dp"),
            P("mp", "dp"),
        ),
        check_vma=False,
    )
```

```python
import functools

import jax
import jax.numpy as jnp
from jax import lax
from jax.experimental import pallas as pl
from jax.experimental.pallas import tpu as pltpu
from jax.sharding import PartitionSpec as P

EROWS = 512


BETA_ONE = 0.9
BETA_TWO = 0.95
LEARN_RATE = 0.02
DECAY_RATE = 0.1
EPSILON = 1e-08
CLIP_NORM = 1.0
AVG_DECAY = 0.9

SUBLANES = 8
LANES = 128
STATE_PARTS = 1
STATE_VMEM = 32 << 20
LATENT_SCALE = 256.0
EMBED_SCALE = 8.0


def embed_partial(token_rows, tok_grads):
    block_rows = EROWS // lax.axis_size("mp")
    slot_ids = lax.axis_index("mp") * block_rows + lax.iota(jnp.int32, block_rows)
    onehot = (slot_ids[:, None] == token_rows[None, :]).astype(jnp.bfloat16)
    return jnp.dot(onehot, tok_grads, preferred_element_type=jnp.float32)


def step_scales(step_count):
    step_float = step_count[0].astype(jnp.float32)
    first_scale = 1.0 / (1.0 - jnp.power(jnp.float32(BETA_ONE), step_float))
    second_scale = 1.0 / (1.0 - jnp.power(jnp.float32(BETA_TWO), step_float))
    return first_scale, second_scale


def clip_factor(sum_squares):
    return CLIP_NORM / jnp.maximum(jnp.sqrt(sum_squares), CLIP_NORM)


def adam(gradient, factor, first_scale, second_scale, master, moment_one, moment_two):
    clipped = factor * gradient
    new_one = BETA_ONE * moment_one + (1.0 - BETA_ONE) * clipped
    new_two = BETA_TWO * moment_two + (1.0 - BETA_TWO) * clipped * clipped
    step = (new_one * first_scale) / (jnp.sqrt(new_two * second_scale) + EPSILON)
    new_master = master - LEARN_RATE * (step + DECAY_RATE * master)
    return new_master, new_one, new_two


def total_factor(squares_ref):
    squares = jnp.sum(squares_ref[...], axis=0, keepdims=True)
    return clip_factor(jnp.sum(squares, axis=1, keepdims=True))


def packed_slots(latent_shape, embed_shape):
    latent_rows, width = latent_shape
    embed_rows, embed_half = embed_shape
    for column in range(0, width, LANES):
        yield False, column, slice(0, latent_rows), slice(column, column + LANES)
    for column in range(0, embed_half, LANES):
        row = latent_rows + column // width * embed_rows
        yield True, column, slice(row, row + embed_rows), slice(column % width, column % width + LANES)


def state_spot(shapes, is_embed, column, side):
    height, half = shapes[is_embed]
    start = shapes[0][0] * 2 * shapes[0][1] // LANES if is_embed else 0
    return pl.ds(start + side * (half // LANES) + column // LANES, height, stride=2 * half // LANES)


def load(sources, targets, sems):
    copies = [pltpu.make_async_copy(*pair, sems.at[i]) for i, pair in enumerate(zip(sources, targets))]
    for copy in copies:
        copy.start()
    for copy in copies:
        copy.wait()


def pick_kernel(shapes, master_ref, one_ref, two_ref, packed_ref, master, one, two, sems):
    load((master_ref, one_ref, two_ref), (master, one, two), sems)
    for is_embed, column, rows, columns in packed_slots(*shapes):
        spot = state_spot(shapes, is_embed, column, lax.axis_index("group"))
        for index, flat_ref in enumerate((master, one, two)):
            packed_ref[index, rows, columns] = flat_ref[spot, :]


def line_steps(me):
    at_end = (me == 0) | (me == 3)
    return jnp.where(at_end, 2, 1), jnp.where(at_end, 1, 2)


def pack_pair(shapes, owner, latent_mine, latent_other, embed, out_ref, latent_scale, embed_scale):
    (latent_rows, half), (embed_rows, embed_half) = shapes
    out_ref[0:latent_rows, :] = (latent_mine.astype(jnp.float32) + latent_other.astype(jnp.float32)) * latent_scale
    spot = pl.ds(pl.multiple_of(owner * embed_rows, embed_rows), embed_rows)
    for column in range(0, embed_half, half):
        row = latent_rows + column // half * embed_rows
        out_ref[row:row + embed_rows, :] = embed[spot, column:column + half] * embed_scale


def across_kernel(shapes, rows_mine, rows_other, latent_mine, latent_other, tok_mine, tok_other,
                  across_ref, embed_ref):
    (latent_rows, half), (_, embed_half) = shapes
    core, owner = lax.axis_index("group"), lax.axis_index("dp") ^ 3
    slots = embed_ref.shape[0]
    ids = lax.axis_index("mp") * slots + lax.broadcasted_iota(jnp.int32, (slots, rows_mine.shape[1]), 0)
    onehots = [(rows[...] == ids).astype(jnp.bfloat16) for rows in (rows_mine, rows_other)]
    columns = pl.ds(pl.multiple_of(core * embed_half, embed_half), embed_half)
    embed_ref[...] = jnp.dot(onehots[0], tok_mine[:, columns], preferred_element_type=jnp.float32) + jnp.dot(
        onehots[1], tok_other[...], preferred_element_type=jnp.float32
    )
    spot = pl.ds(pl.multiple_of(owner * latent_rows, latent_rows), latent_rows)
    columns = pl.ds(pl.multiple_of(core * half, half), half)
    pack_pair(
        shapes, owner, latent_mine[...], latent_other[spot, columns], embed_ref, across_ref, LATENT_SCALE, EMBED_SCALE
    )


def rest_kernel(shapes, latent_mine, latent_other, embed_ref, own_ref, sent_ref):
    latent_rows, half = shapes[0]
    core, me = lax.axis_index("group"), lax.axis_index("dp")
    columns = pl.ds(pl.multiple_of(core * half, half), half)
    for index, step in enumerate((0, *line_steps(me))):
        spot = pl.ds(pl.multiple_of((me ^ step) * latent_rows, latent_rows), latent_rows)
        pack_pair(
            shapes, me ^ step, latent_mine[spot, :], latent_other[spot, columns], embed_ref,
            sent_ref.at[index - 1] if index else own_ref,
            LATENT_SCALE if index else 1.0, EMBED_SCALE if index else 1.0,
        )


def weights_kernel(scale_ref, squares_ref, grad_ref, picked_ref, packed_ref):
    new_master, _, _ = adam(
        grad_ref[...], total_factor(squares_ref), scale_ref[0:1, 0:1], scale_ref[1:2, 0:1],
        picked_ref[0], picked_ref[1], picked_ref[2],
    )
    packed_ref[...] = new_master.astype(packed_ref.dtype)


def state_kernel(shapes, scale_ref, squares_ref, grad_mine, grad_other, *refs):
    sources, targets, (gradient, inside, outside, in_sems, out_sems) = refs[:4], refs[4:8], refs[8:]
    rows = gradient.shape[0] // STATE_PARTS

    def copies(part):
        spot = pl.ds(part * rows, rows)
        return (
            [pltpu.make_async_copy(ref.at[spot], inside.at[i, spot], in_sems.at[part, i]) for i, ref in enumerate(sources)],
            [pltpu.make_async_copy(outside.at[i, spot], ref.at[spot], out_sems.at[part, i]) for i, ref in enumerate(targets)],
        )

    parts = [copies(part) for part in range(STATE_PARTS)]
    for loads, _ in parts:
        for copy in loads:
            copy.start()
    core = lax.axis_index("group")
    for is_embed, column, packed_rows, columns in packed_slots(*shapes):
        for ref, side in ((grad_mine, core), (grad_other, 1 - core)):
            gradient[state_spot(shapes, is_embed, column, side), :] = ref[packed_rows, columns]
    factor = total_factor(squares_ref)
    for part, (loads, stores) in enumerate(parts):
        for copy in loads:
            copy.wait()
        spot = pl.ds(part * rows, rows)
        new_master, new_one, new_two = adam(
            gradient[spot, :], factor, scale_ref[0:1, :], scale_ref[1:2, :], inside[0, spot], inside[1, spot], inside[2, spot]
        )
        outside[0, spot] = new_master
        outside[1, spot] = new_one
        outside[2, spot] = new_two
        outside[3, spot] = AVG_DECAY * inside[3, spot] + (1.0 - AVG_DECAY) * new_master
        for copy in stores:
            copy.start()
    for _, stores in parts:
        for copy in stores:
            copy.wait()


def assemble_kernel(latent_rows, embed_rows, *refs):
    *pieces, latent_out, embed_out = refs
    left_is_mine, me = lax.axis_index("group") == 0, lax.axis_index("dp")
    width = pieces[0].shape[1]
    stretches = (pieces[0].shape[0] - latent_rows) // embed_rows
    second, first = line_steps(me)
    for index, step in enumerate((0, first, second, 3)):
        owner = me ^ step
        latent_spot = pl.ds(pl.multiple_of(owner * latent_rows, latent_rows), latent_rows)
        embed_spot = pl.ds(pl.multiple_of(owner * embed_rows, embed_rows), embed_rows)
        mine, other = pieces[2 * index], pieces[2 * index + 1]

        def put(out_ref, spot, column, rows):
            half = out_ref.shape[1] // 2
            left = jnp.where(left_is_mine, mine[rows, :], other[rows, :])
            right = jnp.where(left_is_mine, other[rows, :], mine[rows, :])
            out_ref[spot, column:column + width] = left
            out_ref[spot, half + column:half + column + width] = right

        put(latent_out, latent_spot, 0, slice(0, latent_rows))
        for stretch in range(stretches):
            row = latent_rows + stretch * embed_rows
            put(embed_out, embed_spot, stretch * width, slice(row, row + embed_rows))


def direct_shards(kv_up_grads, tok_grads, token_rows, step_count, master, moment_one, moment_two, average):
    n_dp = lax.axis_size("dp")
    core, me = lax.axis_index("group"), lax.axis_index("dp")
    swap = [(0, 1), (1, 0)]

    def half_of(array, side):
        half = array.shape[1] // 2
        return lax.dynamic_slice(array, (0, side * half), (array.shape[0], half))

    latent_got = lax.ppermute(kv_up_grads, "group", swap)
    rows_got = lax.ppermute(token_rows, "group", swap)
    tok_got = lax.ppermute(half_of(tok_grads, 1 - core), "group", swap)

    block_rows = EROWS // lax.axis_size("mp")
    shapes = ((kv_up_grads.shape[0] // n_dp, kv_up_grads.shape[1] // 2), (block_rows // n_dp, tok_grads.shape[1] // 2))
    (latent_rows, half), (embed_rows, embed_half) = shapes
    packed_rows = latent_rows + embed_rows * embed_half // half
    states = [array.reshape(-1, LANES) for array in (master, moment_one, moment_two, average)]
    entries = states[0].size

    vmem = pl.BlockSpec(memory_space=pltpu.VMEM)
    hbm = pl.BlockSpec(memory_space=pltpu.HBM)

    packed_shape = jax.ShapeDtypeStruct((packed_rows, half), jnp.float32)
    across_rows = lax.dynamic_slice(kv_up_grads, ((me ^ 3) * latent_rows, core * half), (latent_rows, half))
    across, embed = pl.pallas_call(
        functools.partial(across_kernel, shapes),
        out_shape=[packed_shape, jax.ShapeDtypeStruct((block_rows, embed_half), jnp.float32)],
        in_specs=[vmem] * 6,
        out_specs=[vmem] * 2,
        compiler_params=pltpu.CompilerParams(vmem_limit_bytes=12 << 20),
        name="across",
    )(token_rows.reshape(1, -1), rows_got.reshape(1, -1), across_rows, latent_got, tok_grads, tok_got)
    across = across.astype(jnp.float16)
    across, kv_up_grads = lax.optimization_barrier((across, kv_up_grads))
    across_middle, rows_got = lax.optimization_barrier((across, rows_got))
    own, sent = pl.pallas_call(
        functools.partial(rest_kernel, shapes),
        out_shape=[packed_shape, jax.ShapeDtypeStruct((2, packed_rows, half), jnp.float32)],
        in_specs=[vmem] * 3,
        out_specs=[vmem] * 2,
        compiler_params=pltpu.CompilerParams(vmem_limit_bytes=12 << 20),
        cost_estimate=pl.CostEstimate(flops=4 * entries, bytes_accessed=16 * entries, transcendentals=0),
        name="rest",
    )(half_of(kv_up_grads, core), latent_got, embed)
    early = sent[0].astype(jnp.float16)

    inward, middle, first, second = (
        ((0, 1), (3, 2)), ((1, 2), (2, 1)), ((0, 2), (3, 1), (1, 0), (2, 3)), ((0, 1), (3, 2), (1, 3), (2, 0))
    )

    def send(block, pairs):
        return lax.ppermute(block, "dp", pairs)

    passed = send(across, inward)
    from_middle = send(across_middle, middle)
    from_first = send(early, first)
    late = (sent[1] + passed.astype(jnp.float32)).astype(jnp.float16)
    from_second = send(late, second)

    picked_master, late = lax.optimization_barrier((states[0], late))
    picked = pl.pallas_call(
        functools.partial(pick_kernel, shapes),
        out_shape=jax.ShapeDtypeStruct((3, packed_rows, half), jnp.float32),
        in_specs=[hbm] * 3,
        out_specs=vmem,
        scratch_shapes=[pltpu.VMEM(states[0].shape, jnp.float32)] * 3 + [pltpu.SemaphoreType.DMA((3,))],
        compiler_params=pltpu.CompilerParams(vmem_limit_bytes=8 << 20),
        cost_estimate=pl.CostEstimate(flops=0, bytes_accessed=18 * entries, transcendentals=0),
        name="pick",
    )(picked_master, *states[1:3])

    from_first, picked = lax.optimization_barrier((from_first, picked))
    is_latent = lax.broadcasted_iota(jnp.int32, (packed_rows, 1), 0) < latent_rows
    unscale = jnp.where(is_latent, 1.0 / LATENT_SCALE, 1.0 / EMBED_SCALE)
    gradient = own + (from_middle.astype(jnp.float32) + from_first.astype(jnp.float32)) * unscale
    from_second, gradient = lax.optimization_barrier((from_second, gradient))
    gradient = gradient + from_second.astype(jnp.float32) * unscale
    squares = (gradient * gradient).reshape(-1, SUBLANES, half).sum(axis=0)
    squares = sum(squares[:, i:i + LANES] for i in range(0, half, LANES))
    everyone = ("group", "dp", "mp")
    n_all = lax.axis_size(everyone)
    squares = lax.all_to_all(jnp.tile(squares, (n_all, 1)), everyone, 0, 0, tiled=True)
    scales = jnp.broadcast_to(jnp.stack(step_scales(step_count))[:, None], (2, LANES))

    packed = pl.pallas_call(
        weights_kernel,
        out_shape=jax.ShapeDtypeStruct((packed_rows, half), jnp.bfloat16),
        in_specs=[vmem] * 4,
        out_specs=vmem,
        compiler_params=pltpu.CompilerParams(vmem_limit_bytes=8 << 20),
        name="weights",
)(scales, squares, gradient, picked)

    gradient_other = lax.ppermute(gradient, "group", swap)
    from_first = send(packed, first)
    from_second = send(packed, second)

    state_shape = jax.ShapeDtypeStruct(states[0].shape, jnp.float32)
    new_state = pl.pallas_call(
        functools.partial(state_kernel, shapes),
        out_shape=[state_shape] * 4,
        in_specs=[vmem] * 4 + [hbm] * 4,
        out_specs=[hbm] * 4,
        scratch_shapes=[
            pltpu.VMEM(states[0].shape, jnp.float32),
            pltpu.VMEM((4, *states[0].shape), jnp.float32),
            pltpu.VMEM((4, *states[0].shape), jnp.float32),
            pltpu.SemaphoreType.DMA((STATE_PARTS, 4)),
            pltpu.SemaphoreType.DMA((STATE_PARTS, 4)),
        ],
        compiler_params=pltpu.CompilerParams(vmem_limit_bytes=STATE_VMEM),
        cost_estimate=pl.CostEstimate(flops=30 * entries, bytes_accessed=36 * entries, transcendentals=2 * entries),
        name="state",
    )(scales, squares, gradient, gradient_other, *states)
    packed, new_state = lax.optimization_barrier((packed, new_state))
    from_middle = send(packed, middle)
    from_first, new_state = lax.optimization_barrier((from_first, new_state))
    passed = send(from_first, ((1, 0), (2, 3)))
    inner = (me == 1) | (me == 2)
    gathered = (packed, from_first, from_second, jnp.where(inner, from_middle, passed))
    pieces = []
    for piece in gathered:
        pieces += [piece, lax.ppermute(piece, "group", swap)]
    new_kv_up, new_embed = pl.pallas_call(
        functools.partial(assemble_kernel, latent_rows, embed_rows),
        out_shape=[
            jax.ShapeDtypeStruct(kv_up_grads.shape, jnp.bfloat16),
            jax.ShapeDtypeStruct((n_dp * embed_rows, tok_grads.shape[1]), jnp.bfloat16),
        ],
        in_specs=[vmem] * len(pieces),
        out_specs=[vmem] * 2,
        compiler_params=pltpu.CompilerParams(vmem_limit_bytes=8 << 20),
        name="assemble",
    )(*pieces)
    return (new_kv_up, new_embed, *[array.reshape(master.shape) for array in new_state])


def scattered_shards(kv_up_grads, tok_grads, token_rows, step_count, master, moment_one, moment_two, average):
    latent_part = kv_up_grads.astype(jnp.float32)
    embed_part = embed_partial(token_rows, tok_grads)
    latent_rows, embed_rows = (
        lax.psum_scatter(latent_part, "dp", scatter_dimension=0, tiled=True),
        lax.psum_scatter(embed_part, "dp", scatter_dimension=0, tiled=True),
    )
    latent_rows, embed_rows = lax.psum((latent_rows, embed_rows), "group")
    gradient = jnp.concatenate([latent_rows.reshape(1, -1), embed_rows.reshape(1, -1)], axis=1)
    sum_squares = lax.psum(jnp.sum(gradient * gradient), ("dp", "mp"))
    new_master, new_one, new_two = adam(
        gradient, clip_factor(sum_squares), *step_scales(step_count), master, moment_one, moment_two
    )
    new_average = AVG_DECAY * average + (1.0 - AVG_DECAY) * new_master
    weights = new_master.astype(jnp.bfloat16)
    latent_len = latent_rows.shape[0] * latent_rows.shape[1]
    latent_new = weights[0, :latent_len].reshape(latent_rows.shape)
    embed_new = weights[0, latent_len:].reshape(embed_rows.shape)
    new_kv_up, new_embed = (
        lax.all_gather(latent_new, "dp", axis=0, tiled=True),
        lax.all_gather(embed_new, "dp", axis=0, tiled=True),
    )
    return (new_kv_up, new_embed, new_master, new_one, new_two, new_average)


def solution(mesh):
    placed = (
        P(("group", "dp"), "mp"),
        P(("group", "dp"), None),
        P(("group", "dp")),
        P(),
        P("mp", "dp"),
        P("mp", "dp"),
        P("mp", "dp"),
        P("mp", "dp"),
    )
    in_line = mesh.shape["group"] == 2 and mesh.shape["dp"] == 4
    return jax.shard_map(
        direct_shards if in_line else scattered_shards,
        mesh=mesh,
        in_specs=placed,
        out_specs=(
            P(None, "mp"),
            P("mp", None),
            P("mp", "dp"),
            P("mp", "dp"),
            P("mp", "dp"),
            P("mp", "dp"),
        ),
        check_vma=False,
    )
```
